128 devices in a mesh: dp: 4 (over y), expert: 32 (over x, z, core).
Axes of the slice: x: 4, y: 4, z: 4, core: 2. Of those that a mesh axis runs over, the one named last changes fastest.
Arguments:
- out_grad: bfloat16 [16384, 2880], P(('dp', 'expert')), may hold values from -6 to 6
- expert_ids: int32 [16384, 4], P(('dp', 'expert')), may hold values from 0 to 31, all different within a row; in each aligned block of 128 rows (0 to 127, 128 to 255, ...) at most 20 rows name the same one
- chosen_logits: float32 [16384, 4], P(('dp', 'expert')), may hold values from -6 to 6
- router_weight: bfloat16 [2880, 32], replicated, may hold values from -2 to 2
- hidden_act: bfloat16 [32, 128, 20, 2880], P('expert', None, None, 'dp'), may hold values from -0.29882812 to 0.29882812
- down_weight: bfloat16 [32, 2880, 2880], P('expert', 'dp'), may hold values from -0.109375 to 0.109375
- attn_out: bfloat16 [16384, 2048], P(('dp', 'expert')), may hold values from -6 to 6
- proj_weight: bfloat16 [2048, 2880], P('dp'), may hold values from -0.125 to 0.125
Outputs:
- attn_grad: bfloat16 [16384, 2048], P(('dp', 'expert'))
- proj_grad: bfloat16 [2048, 2880], P('dp')
- down_grad: bfloat16 [32, 2880, 2880], P('expert', 'dp')
- logit_grad: float32 [16384, 4], P(('dp', 'expert'))
The draws below stay inside these ranges and needn't reach their ends.
Inputs may be any that keep to these rules, and one draw needn't show every extreme that they name: `expert_ids`: each token names 4 different experts. Among the tokens of one device no expert is named more than 20 times, and in every draw some expert is named exactly 20 times by the tokens of some device.
All inputs are finite; a program needn't handle non-finite values.
Results may differ from the reference program's by a relative error of at most 0.019.
Values may be sent and summed in bfloat16 or wider, within the bound.
A program may use at most 192 MiB of HBM per device.

```python
import math
import jax
import jax.numpy as jnp
import numpy as np
from jax import lax

D = 2880
FF = 2880
HEADS = 32
HD = 64
TOP = 4
T_DEV = 128
EXPERTS = 32
CAP = 20
TOKENS = 16384
SOURCES = 128
N_DP = 4
N_EXPERT = 32


def steps_of(own_key, dims, pieces, least, largest):
    loudness, own = 1.0, jax.random.fold_in(own_key, 6)
    for dim, parts in pieces:
        draws = jnp.exp(jax.random.uniform(jax.random.fold_in(own, dim), (parts,), jnp.float32, least / len(pieces), largest / len(pieces)))
        loudness = loudness * jnp.repeat(draws, dims[dim] // parts).reshape([-1 if axis == dim else 1 for axis in range(len(dims))])
    return loudness


def assign_block(key, own, number, rows, number_of, top, limit, lean):
    ranking = jax.random.permutation(key, number_of)
    crowded, common = load_shares(number_of, rows * top, limit, lean, True), load_shares(number_of, rows * top, limit, lean, False)
    places = jnp.arange(number_of)

    def named(lengths, offset_by):
        used = int((lengths > 0).sum())
        fixed = max(1, used // 4)
        passed = fixed + (places - fixed + offset_by * (used - fixed)) % max(1, number_of - fixed)
        return jnp.zeros((number_of,), jnp.int32).at[ranking[jnp.where(places < fixed, places, passed)]].set(jnp.asarray(lengths, jnp.int32))

    lengths = jnp.where(number % 4 == 0, named(crowded, number // 4), named(common, number - number // 4 - 1))
    mixed = jax.random.permutation(jax.random.fold_in(own, 3), number_of)
    donor, taker = mixed[0:number_of // 2 * 2:2], mixed[1:number_of // 2 * 2:2]
    room = jnp.minimum(lengths[donor] - 1, limit - lengths[taker]) // 2
    room = jnp.where((donor == ranking[0]) | (taker == ranking[0]) | (lengths[taker] == 0), 0, jnp.maximum(room, 0))
    passed = jax.random.randint(jax.random.fold_in(own, 4), (number_of // 2,), 0, 1 << 20) % (room + 1)
    lengths = lengths.at[donor].add(-passed).at[taker].add(passed)
    labels = jnp.searchsorted(jnp.cumsum(lengths), jnp.arange(rows * top), side="right").astype(jnp.int32)
    table = labels.reshape(top, rows).T
    table = table[jax.random.permutation(jax.random.fold_in(own, 1), rows)]
    offset_by = jax.random.randint(jax.random.fold_in(own, 2), (rows, 1), 0, top)
    return jnp.take_along_axis(table, (jnp.arange(top)[None, :] + offset_by) % top, axis=1)


def load_shares(count, total, limit, slope, full):
    portions = [(1 << 20) // math.isqrt(standing ** slope) + 1 for standing in range(1, count + 1)]
    largest = limit if full else min(limit, max(-(-total // count), total * portions[0] // sum(portions)))
    least = 1 if total - largest >= count - 1 else 0
    counts, surplus = [largest] + [least] * (count - 1), total - largest - least * (count - 1)
    while surplus > 0:
        movable = [i for i in range(1, count) if counts[i] < largest] or [i for i in range(1, count) if counts[i] < limit]
        pool, budget = sum([portions[i] for i in movable]), surplus
        for i in movable:
            addition = min(limit - counts[i], max(1, budget * portions[i] // pool), surplus)
            counts[i] = counts[i] + addition
            surplus = surplus - addition
    return np.array(counts)


def centred(own_key, extent, spread, reach, pieces=(), kind=jnp.bfloat16):
    level = steps_of(own_key, extent, pieces, -0.22, 0.18) if pieces else 1.0
    drawn = jax.random.normal(own_key, extent, jnp.float32) * spread * level
    return jnp.minimum(jnp.maximum(drawn, -reach), reach).astype(kind)


def setup_inputs(seed: int = 0) -> dict:
    streams_of = jax.random.split(jax.random.key(seed), 9)
    out_grad = centred(streams_of[0], (TOKENS, D), 1.0, 6.0, ((0, 128),))
    expert_ids_keys = jax.random.split(jax.random.fold_in(streams_of[1], 1), TOKENS // T_DEV)
    expert_ids_turns = jax.random.permutation(jax.random.fold_in(streams_of[1], 3), TOKENS // T_DEV)
    expert_ids = jax.vmap(lambda own, number: assign_block(jax.random.fold_in(streams_of[1], 2), own, number, T_DEV, EXPERTS, TOP, CAP, 2))(expert_ids_keys, expert_ids_turns).reshape((TOKENS, TOP))
    chosen_logits = centred(streams_of[2], (TOKENS, TOP), 1.5, 6.0, ((0, 128),), jnp.float32)
    router_weight = centred(streams_of[3], (D, EXPERTS), 8 ** -0.5, 2.0)
    hidden_act = centred(streams_of[4], (EXPERTS, SOURCES, CAP, FF), 0.05, 0.29882812, ((0, 32), (3, 4)))
    down_weight = centred(streams_of[5], (EXPERTS, FF, D), FF ** -0.5, 0.109375, ((0, 32), (1, 4)))
    attn_out = centred(streams_of[6], (TOKENS, HEADS * HD), 1.0, 6.0, ((0, 128),))
    proj_weight = centred(streams_of[7], (HEADS * HD, D), (HEADS * HD) ** -0.5, 0.125, ((0, 4),))
    return {"out_grad": out_grad, "expert_ids": expert_ids, "chosen_logits": chosen_logits, "router_weight": router_weight, "hidden_act": hidden_act, "down_weight": down_weight, "attn_out": attn_out, "proj_weight": proj_weight}


def slot_of(ids_flat, experts, cap):
    onehot = (ids_flat[:, None] == jnp.arange(experts, dtype=jnp.int32)[None, :]).astype(jnp.int32)
    before = (jnp.cumsum(onehot, axis=0) - onehot).astype(jnp.int32)
    return (ids_flat * cap + jnp.sum(before * onehot, axis=1)).astype(jnp.int32)


def owner_of(slots, count):
    owner = jnp.full((count,), -1, dtype=jnp.int32)
    return owner.at[slots].set(jnp.arange(slots.shape[0], dtype=jnp.int32))


def reference(out_grad, expert_ids, chosen_logits, router_weight, hidden_act, down_weight, attn_out, proj_weight):
    ndev = N_DP * N_EXPERT
    rows_dev = out_grad.shape[0] // ndev
    width = out_grad.shape[1]
    top = expert_ids.shape[1]
    nexp = down_weight.shape[0]
    cap = hidden_act.shape[2]
    hidden = hidden_act.shape[3]
    expw = jnp.exp(chosen_logits)
    gates = expw / jnp.sum(expw, axis=1, keepdims=True)
    gate_b = gates.astype(jnp.bfloat16)
    ids_dev = expert_ids.reshape(ndev, rows_dev * top)
    slots = jax.vmap(lambda i: slot_of(i, nexp, cap))(ids_dev)
    owners = jax.vmap(lambda s: owner_of(s, nexp * cap))(slots)
    owners_exp = jnp.swapaxes(owners.reshape(ndev, nexp, cap), 0, 1)
    grad_dev = out_grad.reshape(ndev, rows_dev, width)
    gate_dev = gate_b.reshape(ndev, rows_dev * top)

    def per_expert(item):
        own, hid_e, weight = item
        valid = own >= 0
        safe = jnp.maximum(own, 0)
        rows = jax.vmap(lambda g, i: g[i])(grad_dev, safe // top)
        rows = jnp.where(valid[:, :, None], rows, jnp.zeros((), jnp.bfloat16))
        gsl = jax.vmap(lambda g, i: g[i])(gate_dev, safe)
        gsl = jnp.where(valid, gsl, jnp.zeros((), jnp.bfloat16))
        flat = rows.reshape(ndev * cap, width)
        upward = lax.dot_general(flat, weight, (((1,), (1,)), ((), ())), preferred_element_type=jnp.float32)
        hid = hid_e.reshape(ndev * cap, hidden)
        slot_grad = jnp.sum(upward * hid.astype(jnp.float32), axis=1).reshape(ndev, cap)
        scaled = (gsl[:, :, None] * rows).reshape(ndev * cap, width)
        dwd = lax.dot_general(hid, scaled, (((0,), (0,)), ((), ())), preferred_element_type=jnp.float32)
        return slot_grad, dwd.astype(jnp.bfloat16)

    slot_grads, down_grad = lax.map(per_expert, (owners_exp, hidden_act, down_weight))
    slot_dev = jnp.swapaxes(slot_grads, 0, 1).reshape(ndev, nexp * cap)
    choice_grad = jax.vmap(lambda g, i: g[i])(slot_dev, slots).reshape(-1, top)
    logit_grad = gates * (choice_grad - jnp.sum(gates * choice_grad, axis=1, keepdims=True))
    table = (expert_ids[:, :, None] == jnp.arange(nexp, dtype=jnp.int32)[None, None, :]).astype(jnp.float32)
    router_rows = jnp.sum(logit_grad[:, :, None] * table, axis=1).astype(jnp.bfloat16)
    back = lax.dot_general(router_rows, router_weight, (((1,), (1,)), ((), ())), preferred_element_type=jnp.float32)
    resid_grad = (out_grad.astype(jnp.float32) + back).astype(jnp.bfloat16)
    attn_grad = lax.dot_general(resid_grad, proj_weight, (((1,), (1,)), ((), ())), preferred_element_type=jnp.float32).astype(jnp.bfloat16)
    attn_blocks = jnp.swapaxes(attn_out.reshape(N_DP, N_EXPERT, rows_dev, -1), 0, 1)
    resid_blocks = jnp.swapaxes(resid_grad.reshape(N_DP, N_EXPERT, rows_dev, width), 0, 1)

    def add_section(total, item):
        attn_j, resid_j = item
        section = jnp.zeros(total.shape, jnp.float32)
        for p in range(attn_j.shape[0]):
            part = lax.dot_general(attn_j[p], resid_j[p], (((0,), (0,)), ((), ())), preferred_element_type=jnp.float32)
            part = lax.optimization_barrier(part.astype(jnp.bfloat16))
            section = section + part.astype(jnp.float32)
        section = lax.optimization_barrier(section.astype(jnp.bfloat16))
        return total + section.astype(jnp.float32), None

    start = jnp.zeros((attn_out.shape[1], width), jnp.float32)
    total, unused = lax.scan(add_section, start, (attn_blocks, resid_blocks))
    proj_grad = total.astype(jnp.bfloat16)
    return attn_grad, proj_grad, down_grad, logit_grad
```

```python
import functools

import jax
import jax.numpy as jnp
from jax import lax
from jax.experimental import pallas as pl
from jax.experimental.pallas import tpu as pltpu
from jax.sharding import PartitionSpec as P

MESH = pl.DeviceIdType.MESH
BF = jnp.bfloat16
F32 = jnp.float32
D = 2880
DP = 2944
MAIN = 2816
FF = 720
TOK = 128
NE = 32
CAP = 20
SEC = 512
HID = 2048
CH = 256
NA = 8
NC = 3
ROWS = 2560


def dot(a, b, ca, cb, precision=None):
    return lax.dot_general(
        a, b, (((ca,), (cb,)), ((), ())), preferred_element_type=F32, precision=precision
    )


def iota(shape, dim):
    return lax.broadcasted_iota(jnp.int32, shape, dim)


def place():
    y = lax.axis_index("dp")
    e = lax.axis_index("expert")
    x = lax.div(e, 8)
    z = lax.rem(lax.div(e, 2), 4)
    c = lax.rem(e, 2)
    return y, x, z, c


def dev(y, x, z, c):
    return (lax.rem(y, 4), lax.rem(x, 4) * 8 + lax.rem(z, 4) * 2 + c)


def remote(src, dst, ss, rs, to):
    return pltpu.make_async_remote_copy(
        src_ref=src, dst_ref=dst, send_sem=ss, recv_sem=rs, device_id=to, device_id_type=MESH
    )


def greet(peers):
    bar = pltpu.get_barrier_semaphore()
    for p in peers:
        pl.semaphore_signal(bar, inc=1, device_id=p, device_id_type=MESH)
    pl.semaphore_wait(bar, len(peers))


def dense_gates(ids_ref, log_ref):
    lane = iota((TOK, NE), 1)
    w = jnp.exp(log_ref[...])
    gates = w / jnp.sum(w, axis=1, keepdims=True)
    chosen = jnp.zeros((TOK, NE), F32)
    dense = jnp.zeros((TOK, NE), F32)
    for k in range(4):
        hit = ids_ref[:, k : k + 1] == lane
        chosen = chosen + jnp.where(hit, 1.0, 0.0)
        dense = dense + jnp.where(hit, gates[:, k : k + 1], 0.0)
    lower = jnp.where(iota((TOK, TOK), 1) < iota((TOK, TOK), 0), 1.0, 0.0).astype(BF)
    count = dot(lower, chosen.astype(BF), 1, 0)
    pos = jnp.where(chosen > 0.0, count, -1.0)
    return dense, pos


def shift_to(rows, start):
    return jnp.where(iota((rows, 128), 1) == iota((rows, 128), 0) + start, 1.0, 0.0).astype(BF)


def first_kernel(
    og, ids, logits, ao, pw, rw, yt, s1, mr, aos, rpt, ms, aot, rpo, ss, rs, ls
):
    y, x, z, c = place()
    peer = [dev(y + i, x, z, c) for i in (1, 2, 3)]
    dense, pos = dense_gates(ids, logits)
    side = (
        dot(og[:, MAIN:D], shift_to(64, 0), 1, 0)
        + dot(pos.astype(BF), shift_to(NE, 64), 1, 0)
        + dot(dense.astype(BF), shift_to(NE, 96), 1, 0)
    )
    yt[y, :, 0:MAIN] = og[:, 0:MAIN]
    yt[y, :, MAIN:DP] = side.astype(BF)
    greet(peer)

    def tok(i):
        return remote(yt.at[y], yt.at[y], ss.at[i], rs.at[i], peer[0 if i == 0 else 2])

    def fwd(i):
        src = lax.rem(y + (3 if i == 0 else 1), 4)
        part = yt.at[src, pl.ds(64 * i, 64)]
        return remote(part, part, ss.at[2 + i], rs.at[2 + i], peer[0 if i == 0 else 2])

    def sections(i):
        to = lax.rem(y + i + 1, 4)
        cols = pl.ds(pl.multiple_of(to * SEC, SEC), SEC)
        return remote(ao.at[:, cols], aos.at[y], ss.at[4 + i], rs.at[4 + i], peer[i])

    def rp(i):
        return remote(rpo, rpt.at[y], ss.at[7 + i], rs.at[7 + i], peer[i])

    def back(i):
        to = lax.rem(y + i + 1, 4)
        return remote(ms.at[to], mr.at[y], ss.at[10 + i], rs.at[10 + i], peer[i])

    tok(0).start()
    tok(1).start()
    for i in range(3):
        sections(i).start()
    own = pltpu.make_async_copy(
        ao.at[:, pl.ds(pl.multiple_of(y * SEC, SEC), SEC)], aos.at[y], ls.at[0]
    )
    own.start()
    rpo[...] = dot(pw[...], rw[...], 1, 0).astype(BF)
    for i in range(3):
        rp(i).start()
    rpt[y] = rpo[...]

    def proj(t):
        return dot(yt[t, :, 0:D], pw[...], 1, 1).astype(BF)

    mr[y] = proj(y)
    tok(0).wait_recv()
    fwd(0).start()
    tok(1).wait_recv()
    fwd(1).start()
    for i in (0, 2):
        to = lax.rem(y + i + 1, 4)
        ms[to] = proj(to)
        back(i).start()
    own.wait()
    for i in range(3):
        sections(i).wait_recv()
    eye = jnp.where(iota((SEC, SEC), 0) == iota((SEC, SEC), 1), 1.0, 0.0).astype(BF)
    for t in range(4):
        aot[:, t * TOK : (t + 1) * TOK] = dot(eye, aos[t], 1, 1).astype(BF)
    fwd(0).wait_recv()
    fwd(1).wait_recv()
    to = lax.rem(y + 2, 4)
    ms[to] = proj(to)
    back(1).start()

    @pl.loop(0, MAIN // CH)
    def _(k):
        cols = pl.ds(pl.multiple_of(k * CH, CH), CH)
        block = yt[:, :, cols].reshape(4 * TOK, CH)
        s1[:, cols] = dot(aot[...], block, 1, 0).astype(BF)

    last = yt[:, :, MAIN:DP].reshape(4 * TOK, 128)
    s1[:, MAIN:D] = dot(aot[...], last, 1, 0)[:, 0:64].astype(BF)
    for i in range(2):
        tok(i).wait_send()
        fwd(i).wait_send()
    for i in range(3):
        sections(i).wait_send()
        rp(i).wait()
        back(i).wait()


def second_kernel(
    yt, hid_h, w_h, ids, logits, mr, aos, rpt,
    dg, attn, lg, qt,
    za, zc, zs, sb, sa, sc, sss, ra, rc, rsd, w, hid, hgt, acc, stg, stl,
    vs, yr, xr, zr, cr, rr, q0, q1, q2, q3,
    a_s, a_r, c_s, c_r, t_s, t_r, ls,
):
    y, x, z, c = place()
    e = x * 8 + z * 2 + c
    zp = [dev(y, x, z + i, c) for i in (1, 2, 3)]
    xp = [dev(y, x + i, z, c) for i in (1, 2, 3)]
    yp = [dev(y + i, x, z, c) for i in (1, 2, 3)]
    cp = dev(y, x, z, 1 - c)
    in_w = pltpu.make_async_copy(w_h, w, ls.at[0])
    in_h = pltpu.make_async_copy(hid_h, hid, ls.at[1])
    in_w.start()
    in_h.start()
    greet(zp + xp + yp + [cp])

    def src_rows(zz, cc):
        return pl.ds(pl.multiple_of((zz * 2 + cc) * TOK, TOK), TOK)

    mine = src_rows(z, c)

    def cols_of(k):
        return pl.ds(pl.multiple_of(k * CH, CH), CH)

    def a_z(k, i):
        src = yt.at[y, :, cols_of(k)]
        to = cp if i == 3 else zp[i]
        return remote(src, za.at[k, mine], a_s.at[k, i], a_r.at[k, i], to)

    def a_own(k):
        return pltpu.make_async_copy(yt.at[y, :, cols_of(k)], za.at[k, mine], a_s.at[k, 14])

    def a_c(k, i):
        part = za.at[k, src_rows(lax.rem(z + 3 - i, 4), c)]
        return remote(part, part, a_s.at[k, 4 + i], a_r.at[k, 4 + i], cp)

    def x_rows(yy, xx):
        return pl.ds(pl.multiple_of(yy * 640 + xx * 160, 160), 160)

    def a_x(k, i):
        to = lax.rem(x + i + 1, 4)
        return remote(
            sa.at[k, to], ra.at[k, x_rows(y, x)], a_s.at[k, 7 + i], a_r.at[k, 7 + i], xp[i]
        )

    def a_xown(k):
        return pltpu.make_async_copy(sa.at[k, x], ra.at[k, x_rows(y, x)], a_s.at[k, 15])

    def a_y(k, i):
        part = ra.at[k, pl.ds(pl.multiple_of(y * 640, 640), 640)]
        return remote(part, part, a_s.at[k, 10 + i], a_r.at[k, 10 + i], yp[2 * i])

    def a_f(k, i):
        src = lax.rem(y + (3 if i == 0 else 1), 4)
        part = ra.at[k, pl.ds(pl.multiple_of(src * 640 + 320 * i, 320), 320)]
        return remote(part, part, a_s.at[k, 12 + i], a_r.at[k, 12 + i], yp[2 * i])

    def c_refs(j, tail):
        if tail:
            return yt.at[:, :, pl.ds(MAIN, 128)], zs, sss, rsd
        return yt.at[:, :, cols_of(NA + j)], zc.at[j], sc.at[j], rc.at[j]

    def c_z(j, i, tail=False):
        src, zb, _, _ = c_refs(j, tail)
        to = cp if i == 3 else zp[i]
        return remote(src, zb.at[:, mine], c_s.at[j, i], c_r.at[j, i], to)

    def c_own(j, tail=False):
        src, zb, _, _ = c_refs(j, tail)
        return pltpu.make_async_copy(src, zb.at[:, mine], c_s.at[j, 14])

    def c_c(j, i, tail=False):
        _, zb, _, _ = c_refs(j, tail)
        part = zb.at[:, src_rows(lax.rem(z + 3 - i, 4), c)]
        return remote(part, part, c_s.at[j, 4 + i], c_r.at[j, 4 + i], cp)

    def c_x(j, i, tail=False):
        _, _, sbuf, rbuf = c_refs(j, tail)
        to = lax.rem(x + i + 1, 4)
        return remote(
            sbuf.at[to], rbuf.at[:, x], c_s.at[j, 7 + i], c_r.at[j, 7 + i], xp[i]
        )

    def c_xown(j, tail=False):
        _, _, sbuf, rbuf = c_refs(j, tail)
        return pltpu.make_async_copy(sbuf.at[x], rbuf.at[:, x], c_s.at[j, 15])

    def picks(yy):
        row, lane = iota((8, 128), 0), iota((8, 128), 1)
        sel = jnp.where((lane == 64 + row * 8 + z * 2 + c) & (row < 4), 1.0, 0.0).astype(BF)
        pos = dot(sel, zs[yy], 1, 1)
        r, t = iota((160, 1024), 0), iota((160, 1024), 1)
        base = jnp.zeros((160, 1024), jnp.int32)
        for s in range(1, 8):
            base = base + jnp.where(r >= s * CAP, 1, 0)
        key = jnp.where(lax.shift_right_logical(t, 7) == base, r - base * CAP, -5).astype(F32)
        for xx in range(4):
            one = jnp.where(pos[xx : xx + 1, :] == key, 1.0, 0.0).astype(BF)
            sb[yy, xx * 160 : (xx + 1) * 160, :] = one

    def send_c(j, tail=False):
        _, zb, sbuf, _ = c_refs(j, tail)

        @pl.loop(0, 4)
        def _(yy):
            got = dot(sb[yy], zb[yy], 1, 0).astype(BF)
            for xx in range(4):
                sbuf[xx, yy] = got[xx * 160 : (xx + 1) * 160]

        for i in range(3):
            c_x(j, i, tail).start()
        c_xown(j, tail).start()

    def slot_part(rows, cols, width):
        @pl.loop(0, 4)
        def _(b):
            rb = pl.ds(pl.multiple_of(b * 640, 640), 640)
            g = dot(hid[rb, :], w[:, cols], 1, 0)
            prod = g * rows[rb].astype(F32)
            if width == CH:
                acc[rb, :] += prod[:, 0:128] + prod[:, 128:256]
            else:
                acc[rb, 0:width] += prod

    def put(slot, k):
        return pltpu.make_async_copy(stg.at[slot], dg.at[:, cols_of(k)], ls.at[2 + slot])

    def put_tail():
        return pltpu.make_async_copy(stl, dg.at[:, pl.ds(MAIN, 128)], ls.at[4])

    @pl.loop(-4, NA + 2)
    def _(t):
        @pl.when((t >= 0) & (t < NA))
        def _():
            a_xown(t).wait()
            for i in range(3):
                a_x(t, i).wait_recv()
            for i in range(2):
                a_y(t, i).start()

        @pl.when((t >= 1) & (t < NA + 1))
        def _():
            for i in range(2):
                a_y(t - 1, i).wait_recv()
                a_f(t - 1, i).start()

        @pl.when(t == -4)
        def _():
            for i in range(4):
                c_z(NC, i, True).start()
            c_own(NC, True).start()

        @pl.when(t == -3)
        def _():
            for i in range(3):
                c_z(NC, i, True).wait_recv()
                c_c(NC, i, True).start()

        @pl.when(t == -2)
        def _():
            c_own(NC, True).wait()
            c_z(NC, 3, True).wait_recv()
            for i in range(3):
                c_c(NC, i, True).wait_recv()
            picks(y)

        @pl.when((t >= -2) & (t < NA - 2))
        def _():
            k = t + 2
            a_own(k).wait()
            a_z(k, 3).wait_recv()
            for i in range(3):
                a_c(k, i).wait_recv()
            got = dot(sb[y], za[k], 1, 0).astype(BF)
            for xx in range(4):
                sa[k, xx] = got[xx * 160 : (xx + 1) * 160]
            for i in range(3):
                a_x(k, i).start()
            a_xown(k).start()

        @pl.when((t >= -3) & (t < NA - 3))
        def _():
            for i in range(3):
                a_z(t + 3, i).wait_recv()
                a_c(t + 3, i).start()

        @pl.when((t >= -4) & (t < NA - 4))
        def _():
            for i in range(4):
                a_z(t + 4, i).start()
            a_own(t + 4).start()

        @pl.when(t == -1)
        def _():
            for i in (1, 2, 3):
                picks(lax.rem(y + i, 4))
            send_c(NC, True)
            in_w.wait()
            in_h.wait()
            acc[...] = jnp.zeros_like(acc)
            eye = jnp.where(iota((FF, FF), 0) == iota((FF, FF), 1), 1.0, 0.0).astype(BF)

            @pl.loop(0, ROWS // 256)
            def _(b):
                rb = pl.ds(pl.multiple_of(b * 256, 256), 256)
                hgt[:, rb] = dot(eye, hid[rb, :], 1, 1).astype(BF)

        @pl.when(t == 1)
        def _():
            c_xown(NC, True).wait()
            for i in range(3):
                c_x(NC, i, True).wait_recv()
            rows = rsd[...].reshape(ROWS, 128)
            sel = jnp.where(iota((8, 128), 1) == 96 + e, 1.0, 0.0).astype(BF)
            gate = dot(sel, rows, 1, 1)[0:1, :]

            @pl.loop(0, FF // 16)
            def _(b):
                rb = pl.ds(pl.multiple_of(b * 16, 16), 16)
                hgt[rb, :] = (hgt[rb, :].astype(F32) * gate).astype(BF)

            stl[...] = dot(hgt[...], rows, 1, 0).astype(BF)
            put_tail().start()
            g = dot(hid[...], w[:, MAIN:D], 1, 0)
            acc[:, 0:64] += g * rows[:, 0:64].astype(F32)

        odd = lax.rem(t + 8, 2) == 1
        j0 = lax.div(t + 1, 2)
        j2 = lax.div(t - 1, 2)

        @pl.when(odd & (t >= -1) & (j0 < NC))
        def _():
            for i in range(4):
                c_z(j0, i).start()
            c_own(j0).start()

        @pl.when(jnp.logical_not(odd) & (t >= 0) & (lax.div(t, 2) < NC))
        def _():
            j1 = lax.div(t, 2)
            for i in range(3):
                c_z(j1, i).wait_recv()
                c_c(j1, i).start()

        @pl.when(odd & (t >= 1) & (j2 < NC))
        def _():
            c_own(j2).wait()
            c_z(j2, 3).wait_recv()
            for i in range(3):
                c_c(j2, i).wait_recv()
            send_c(j2)

        @pl.when(odd & (t >= 3) & (t < 3 + 2 * NC))
        def _():
            j = lax.div(t - 3, 2)
            c_xown(j).wait()
            for i in range(3):
                c_x(j, i).wait_recv()

            @pl.when(j > 0)
            def _():
                put(1, NA + j - 1).wait()

            stg[1] = dot(hgt[...], rc[j].reshape(ROWS, CH), 1, 0).astype(BF)
            put(1, NA + j).start()

            @pl.loop(0, 4)
            def _(b):
                rb = pl.ds(pl.multiple_of(b * 640, 640), 640)
                g = dot(hid[rb, :], w[:, cols_of(NA + j)], 1, 0)
                prod = g * rc[j, b].reshape(640, CH).astype(F32)
                acc[rb, :] += prod[:, 0:128] + prod[:, 128:256]

        @pl.when((t >= 2) & (t < NA + 2))
        def _():
            k = t - 2
            for i in range(2):
                a_f(k, i).wait_recv()

            @pl.when(k > 0)
            def _():
                put(0, k - 1).wait()

            stg[0] = dot(hgt[...], ra[k], 1, 0).astype(BF)
            put(0, k).start()

            @pl.loop(0, 4)
            def _(b):
                rb = pl.ds(pl.multiple_of(b * 640, 640), 640)
                g = dot(hid[rb, :], w[:, cols_of(k)], 1, 0)
                prod = g * ra[k, rb, :].astype(F32)
                acc[rb, :] += prod[:, 0:128] + prod[:, 128:256]

    exact = lax.Precision.HIGHEST
    r1 = iota((160, 128), 0)
    base = jnp.zeros((160, 128), jnp.int32)
    for s in range(1, 8):
        base = base + jnp.where(r1 >= s * CAP, 1, 0)
    at_slot = iota((160, 128), 1) == r1 - base * CAP
    r2 = iota((8, 160), 1)
    low = iota((8, 160), 0) * CAP
    fold = jnp.where((r2 >= low) & (r2 < low + CAP), 1.0, 0.0)
    for b in range(16):
        total = jnp.sum(acc[b * 160 : (b + 1) * 160, :], axis=1, keepdims=True)
        vs[b // 4, b % 4] = dot(fold, jnp.where(at_slot, total, 0.0), 1, 0, exact)

    def s_y(i):
        return remote(
            vs.at[lax.rem(y + i + 1, 4)], yr.at[i], t_s.at[i], t_r.at[i], yp[i]
        )

    def s_x(i):
        to = lax.rem(x + i + 1, 4)
        return remote(vs.at[0, to], xr.at[x], t_s.at[3 + i], t_r.at[3 + i], xp[i])

    def s_z(i):
        return remote(xr, zr.at[:, z], t_s.at[6 + i], t_r.at[6 + i], zp[i])

    def s_c():
        return remote(zr, cr.at[:, :, c], t_s.at[9], t_r.at[9], cp)

    def r_y(i):
        return remote(rr.at[y], rr.at[y], t_s.at[10 + i], t_r.at[10 + i], yp[i])

    def q_c():
        return remote(q0, q1, t_s.at[13], t_r.at[13], cp)

    def q_z(i):
        return remote(q2.at[0], q2.at[1 + i], t_s.at[14 + i], t_r.at[14 + i], zp[i])

    def q_x(i):
        return remote(q3.at[0], q3.at[1 + i], t_s.at[17 + i], t_r.at[17 + i], xp[i])

    for i in range(3):
        s_y(i).start()
    dense, pos = dense_gates(ids, logits)
    for i in range(3):
        s_y(i).wait()
    vs[0] = vs[y] + yr[0] + yr[1] + yr[2]
    for i in range(3):
        s_x(i).start()
    xr[x] = vs[0, x]
    for i in range(3):
        s_x(i).wait()
    for i in range(3):
        s_z(i).start()
    zr[:, z] = xr[...]
    for i in range(3):
        s_z(i).wait()
    s_c().start()
    cr[:, :, c] = zr[...]
    s_c().wait()
    got = cr[...].reshape(NE, 8, 128)
    got = jnp.sum(jnp.where(iota((NE, 8, 128), 1) == z * 2 + c, got, 0.0), axis=1)
    back = jnp.transpose(jnp.concatenate([got, jnp.zeros((96, 128), F32)], axis=0))
    grad = jnp.zeros((TOK, NE), F32)
    for s in range(CAP):
        grad = grad + jnp.where(pos == s, back[s : s + 1, 0:NE], 0.0)
    inner = jnp.sum(dense * grad, axis=1, keepdims=True)
    full = dense * (grad - inner)
    rrow = dot(full.astype(BF), shift_to(NE, 0), 1, 0).astype(BF)
    rr[y] = rrow
    for i in range(3):
        r_y(i).start()
    lane = iota((TOK, NE), 1)
    for k in range(4):
        hit = ids[:, k : k + 1] == lane
        lg[:, k : k + 1] = jnp.sum(jnp.where(hit, full, 0.0), axis=1, keepdims=True)
    for i in range(3):
        r_y(i).wait()
    q = jnp.zeros((NE, SEC), F32)
    for t in range(4):
        q = q + dot(rr[t], aos[t], 0, 0)[0:NE]
    q0[...] = q
    q_c().start()
    for t in range(4):
        more = dot(rrow[:, 0:NE], rpt[t], 1, 1)
        attn[:, t * SEC : (t + 1) * SEC] = (mr[t].astype(F32) + more).astype(BF)
    q_c().wait()
    q2[0] = q0[...] + q1[...]
    for i in range(3):
        q_z(i).start()
    for i in range(3):
        q_z(i).wait()
    q3[0] = (q2[0] + q2[1]) + (q2[2] + q2[3])
    for i in range(3):
        q_x(i).start()
    for i in range(3):
        q_x(i).wait()
    qt[...] = (q3[0] + q3[1]) + (q3[2] + q3[3])

    put(0, NA - 1).wait()
    put(1, NA + NC - 1).wait()
    put_tail().wait()

    @pl.loop(0, NA)
    def _(k):
        for i in range(4):
            a_z(k, i).wait_send()
        for i in range(3):
            a_c(k, i).wait_send()
            a_x(k, i).wait_send()
        for i in range(2):
            a_y(k, i).wait_send()
            a_f(k, i).wait_send()

    def drain(j, tail):
        for i in range(4):
            c_z(j, i, tail).wait_send()
        for i in range(3):
            c_c(j, i, tail).wait_send()
            c_x(j, i, tail).wait_send()

    @pl.loop(0, NC)
    def _(j):
        drain(j, False)

    drain(NC, True)


def local(
    out_grad, expert_ids, chosen_logits, router_weight, hidden_act, down_weight, attn_out, proj_weight
):
    vm = pl.BlockSpec(memory_space=pltpu.VMEM)
    hbm = pl.BlockSpec(memory_space=pl.ANY)
    sds = jax.ShapeDtypeStruct
    sem = pltpu.SemaphoreType.DMA
    yt, s1, mr, aos, rpt = pl.pallas_call(
        first_kernel,
        out_shape=(
            sds((4, TOK, DP), BF), sds((SEC, D), BF), sds((4, TOK, SEC), BF),
            sds((4, TOK, SEC), BF), sds((4, SEC, NE), BF),
        ),
        in_specs=[vm, vm, vm, hbm, vm, vm],
        out_specs=(vm,) * 5,
        scratch_shapes=[
            pltpu.VMEM((4, TOK, SEC), BF), pltpu.VMEM((SEC, SEC), BF), pltpu.VMEM((SEC, NE), BF),
            sem((13,)), sem((13,)), sem((1,)),
        ],
        compiler_params=pltpu.CompilerParams(
            collective_id=0, has_side_effects=True, vmem_limit_bytes=40 * 2**20
        ),
        cost_estimate=pl.CostEstimate(
            flops=7 * 10**9, bytes_accessed=16 * 10**6, transcendentals=0
        ),
        name="first",
    )(out_grad, expert_ids, chosen_logits, attn_out, proj_weight, router_weight)
    total = lax.psum(s1, "expert")
    hid = hidden_act[0].reshape(ROWS, FF)
    v = pltpu.VMEM
    dg, attn, lg, qt = pl.pallas_call(
        second_kernel,
        out_shape=(
            sds((FF, DP), BF), sds((TOK, HID), BF), sds((TOK, 4), F32), sds((NE, SEC), F32),
        ),
        in_specs=[hbm, hbm, hbm, vm, vm, vm, vm, vm],
        out_specs=(hbm, vm, vm, vm),
        scratch_shapes=[
            v((NA, 1024, CH), BF), v((NC, 4, 1024, CH), BF), v((4, 1024, 128), BF),
            v((4, 640, 1024), BF), v((NA, 4, 160, CH), BF), v((NC, 4, 4, 160, CH), BF),
            v((4, 4, 160, 128), BF), v((NA, ROWS, CH), BF), v((NC, 4, 4, 160, CH), BF),
            v((4, 4, 160, 128), BF), v((FF, D), BF), v((ROWS, FF), BF), v((FF, ROWS), BF),
            v((ROWS, 128), F32), v((2, FF, CH), BF), v((FF, 128), BF),
            v((4, 4, 8, 128), F32), v((3, 4, 8, 128), F32), v((4, 8, 128), F32),
            v((4, 4, 8, 128), F32), v((4, 4, 2, 8, 128), F32), v((4, TOK, 128), BF),
            v((NE, SEC), F32), v((NE, SEC), F32), v((4, NE, SEC), F32), v((4, NE, SEC), F32),
            sem((NA, 16)), sem((NA, 16)), sem((NC + 1, 16)), sem((NC + 1, 16)),
            sem((20,)), sem((20,)), sem((5,)),
        ],
        compiler_params=pltpu.CompilerParams(
            collective_id=1, has_side_effects=True, vmem_limit_bytes=62 * 2**20
        ),
        cost_estimate=pl.CostEstimate(
            flops=50 * 10**9, bytes_accessed=400 * 10**6, transcendentals=0
        ),
        name="second",
    )(yt, hid, down_weight[0], expert_ids, chosen_logits, mr, aos, rpt)
    more = dot(qt.astype(BF), router_weight, 0, 1)
    proj_grad = (total.astype(F32) + more).astype(BF)
    return attn, proj_grad, dg[:, :D][None], lg


def solution(mesh):
    return jax.shard_map(
        local,
        mesh=mesh,
        in_specs=(
            P(("dp", "expert"), None),
            P(("dp", "expert"), None),
            P(("dp", "expert"), None),
            P(),
            P("expert", None, None, "dp"),
            P("expert", "dp", None),
            P(("dp", "expert"), None),
            P("dp", None),
        ),
        out_specs=(
            P(("dp", "expert"), None),
            P("dp", None),
            P("expert", "dp", None),
            P(("dp", "expert"), None),
        ),
        check_vma=False,
    )
```

```python
import functools

import jax
import jax.numpy as jnp
from jax import lax
from jax.experimental import pallas as pl
from jax.experimental.pallas import tpu as pltpu
from jax.sharding import PartitionSpec as P

MESH = pl.DeviceIdType.MESH
BF = jnp.bfloat16
F32 = jnp.float32
D = 2880
DP = 2944
MAIN = 2816
FF = 720
TOK = 128
NE = 32
CAP = 20
SEC = 512
HID = 2048
CH = 256
NA = 7
NC = 4
CB = NA * CH
STEPS = 28
AT = {
    "gate_hidden": (18,),
    "tail_core": (10,),
    "a_core": (2, 3, 4, 7, 8, 13, 14),
    "a_work": (21, 22, 23, 24, 25, 26, 27),
    "send_sections": (4,),
    "attn_part": (17,),
    "known_part": (14,),
    "tail_pick": (11,),
    "a_send_z": (0, 1, 2, 4, 5, 7, 8),
    "tail_z": (5,),
    "tok_c_ring": (2,),
    "tok_a_send": (2,),
    "y_send": (7, 8, 9, 10, 11, 19, 20),
    "c_work": (20, 21, 24, 27),
    "c_core": (12, 15, 18, 24),
    "sum_core": (17,),
    "pack_hidden": (1,),
    "c_pick": (13, 17, 20, 25),
    "give_z": (25,),
    "give_core": (27,),
    "y_ring": (11, 15, 16, 17, 18, 24, 25),
    "sum_x": (24,),
    "c_send_z": (5, 12, 16, 18),
    "sum_z": (22,),
    "tok_a_ring": (8,),
    "pick_own": (2,),
    "tail_own_core": (1,),
    "a_pick": (2, 5, 6, 7, 8, 13, 14),
}
ROWS = 2560


def dot(a, b, ca, cb, precision=None):
    return lax.dot_general(
        a, b, (((ca,), (cb,)), ((), ())), preferred_element_type=F32, precision=precision
    )


def iota(shape, dim):
    return lax.broadcasted_iota(jnp.int32, shape, dim)


def place():
    y = lax.axis_index("dp")
    e = lax.axis_index("expert")
    x = lax.div(e, 8)
    z = lax.rem(lax.div(e, 2), 4)
    c = lax.rem(e, 2)
    return y, x, z, c


def dev(y, x, z, c):
    return (lax.rem(y, 4), lax.rem(x, 4) * 8 + lax.rem(z, 4) * 2 + c)


def remote(src, dst, ss, rs, to):
    return pltpu.make_async_remote_copy(
        src_ref=src, dst_ref=dst, send_sem=ss, recv_sem=rs, device_id=to, device_id_type=MESH
    )


def greet(peers):
    bar = pltpu.get_barrier_semaphore()
    for p in peers:
        pl.semaphore_signal(bar, inc=1, device_id=p, device_id_type=MESH)
    pl.semaphore_wait(bar, len(peers))


def dense_gates(ids, logits):
    row = iota((NE, TOK), 0)
    w = jnp.exp(logits[...])
    gates = w / jnp.sum(w, axis=0, keepdims=True)
    chosen = jnp.zeros((NE, TOK), F32)
    dense = jnp.zeros((NE, TOK), F32)
    for k in range(4):
        hit = ids[k : k + 1, :] == row
        chosen = chosen + jnp.where(hit, 1.0, 0.0)
        dense = dense + jnp.where(hit, gates[k : k + 1, :], 0.0)
    upper = jnp.where(iota((TOK, TOK), 0) < iota((TOK, TOK), 1), 1.0, 0.0).astype(BF)
    count = dot(chosen.astype(BF), upper, 1, 0)
    return dense, jnp.where(chosen > 0.0, count, -1.0)


def eye(n):
    return jnp.where(iota((n, n), 0) == iota((n, n), 1), 1.0, 0.0).astype(BF)


def kernel(
    og_h, ids_h, log_h, ao, pw_h, rw_h, hid_h, w_h,
    dg, total, ra, rc, attn, lg, qt,
    og, ids, logits, pw, rw, hp, yt, za, zc, zs, sb, sa, sc, sss, rsd, rbuf, w, hid, hgt, acc,
    stg, stl, aos, aot, ms, mr, rpo, rpt, s1, cb, zb_, p1, xb_, xg,
    vs, yr, xr, zr, cr, rr, q0, q1, q2, q3,
    a_s, a_r, c_s, c_r, k_s, k_r, g_s, g_r, t_s, t_r, ls,
):
    y, x, z, c = place()
    e = x * 8 + z * 2 + c
    zp = [dev(y, x, z + i, c) for i in (1, 2, 3)]
    xp = [dev(y, x + i, z, c) for i in (1, 2, 3)]
    yp = [dev(y + i, x, z, c) for i in (1, 2, 3)]
    cp = dev(y, x, z, 1 - c)
    loads = [
        pltpu.make_async_copy(a, b, ls.at[5 + n])
        for n, (a, b) in enumerate(
            [(og_h, og), (ids_h, ids), (log_h, logits), (rw_h, rw), (pw_h, pw), (w_h, w)]
        )
    ]

    def load_hid(b):
        return pltpu.make_async_copy(
            hid_h.at[pl.ds(b * 2, 2)], hp.at[lax.rem(b, 2)], ls.at[11 + lax.rem(b, 2)]
        )

    for l in loads:
        l.start()
    load_hid(0).start()
    load_hid(1).start()
    greet(zp + xp + yp + [cp])
    for l in loads[:3]:
        l.wait()
    dense, pos = dense_gates(ids, logits)
    side = [og[MAIN:D, :], pos.astype(BF), dense.astype(BF)]
    yt[0, :, MAIN:DP] = dot(eye(TOK), jnp.concatenate(side, axis=0), 1, 1).astype(BF)

    @pl.loop(0, MAIN // CH)
    def _(k):
        rows = pl.ds(pl.multiple_of(k * CH, CH), CH)
        yt[0, :, rows] = dot(eye(TOK), og[rows, :], 1, 1).astype(BF)

    def src_rows(zz, cc):
        return pl.ds(pl.multiple_of((zz * 2 + cc) * TOK, TOK), TOK)

    mine = src_rows(z, c)

    def cols_of(k):
        return pl.ds(pl.multiple_of(k * CH, CH), CH)

    def tok(part, i):
        cols = pl.ds(CB, DP - CB) if part == 0 else pl.ds(0, CB)
        n = part * 4 + i
        return remote(
            yt.at[0, :, cols], yt.at[3 if i == 0 else 1, :, cols], k_s.at[n], k_r.at[n], yp[2 * i]
        )

    def tok_f(part, i):
        cols = pl.ds(CB, DP - CB) if part == 0 else pl.ds(0, CB)
        n = part * 4 + 2 + i
        rows = pl.ds(64 * i, 64)
        return remote(
            yt.at[3 if i == 0 else 1, rows, cols], yt.at[2, rows, cols],
            k_s.at[n], k_r.at[n], yp[2 * i],
        )

    def sections(i):
        to = lax.rem(y + i + 1, 4)
        cols = pl.ds(pl.multiple_of(to * SEC, SEC), SEC)
        return remote(ao.at[:, cols], aos.at[3 - i], k_s.at[8 + i], k_r.at[8 + i], yp[i])

    def own_section():
        cols = pl.ds(pl.multiple_of(y * SEC, SEC), SEC)
        return pltpu.make_async_copy(ao.at[:, cols], aos.at[0], ls.at[13])

    def rp(i):
        return remote(rpo, rpt.at[y], k_s.at[11 + i], k_r.at[11 + i], yp[i])

    def back(i):
        return remote(ms.at[i], mr.at[y], k_s.at[14 + i], k_r.at[14 + i], yp[i])

    def a_z(k, i):
        to = cp if i == 3 else zp[i]
        return remote(
            yt.at[0, :, cols_of(k)], za.at[k, mine], a_s.at[k, i], a_r.at[k, i], to
        )

    def a_own(k):
        return pltpu.make_async_copy(yt.at[0, :, cols_of(k)], za.at[k, mine], a_s.at[k, 14])

    def a_c(k, i):
        part = za.at[k, src_rows(lax.rem(z + 3 - i, 4), c)]
        return remote(part, part, a_s.at[k, 4 + i], a_r.at[k, 4 + i], cp)

    def x_rows(yy, xx):
        return pl.ds(pl.multiple_of(yy * 640 + xx * 160, 160), 160)

    def a_x(k, i):
        to = lax.rem(x + i + 1, 4)
        return remote(
            sa.at[k, to], ra.at[k, x_rows(y, x)], a_s.at[k, 7 + i], a_r.at[k, 7 + i], xp[i]
        )

    def a_xown(k):
        return pltpu.make_async_copy(sa.at[k, x], ra.at[k, x_rows(y, x)], a_s.at[k, 15])

    def a_y(k, i):
        part = ra.at[k, pl.ds(pl.multiple_of(y * 640, 640), 640)]
        return remote(part, part, a_s.at[k, 10 + i], a_r.at[k, 10 + i], yp[2 * i])

    def a_f(k, i):
        src = lax.rem(y + (3 if i == 0 else 1), 4)
        part = ra.at[k, pl.ds(pl.multiple_of(src * 640 + 320 * i, 320), 320)]
        return remote(part, part, a_s.at[k, 12 + i], a_r.at[k, 12 + i], yp[2 * i])

    def c_z(j, i):
        to = cp if i == 3 else zp[i]
        return remote(
            yt.at[:, :, cols_of(NA + j)], zc.at[j, :, mine], c_s.at[j, i], c_r.at[j, i], to
        )

    def c_own(j):
        return pltpu.make_async_copy(
            yt.at[:, :, cols_of(NA + j)], zc.at[j, :, mine], c_s.at[j, 14]
        )

    def c_c(j, i):
        part = zc.at[j, :, src_rows(lax.rem(z + 3 - i, 4), c)]
        return remote(part, part, c_s.at[j, 4 + i], c_r.at[j, 4 + i], cp)

    def c_x(j, i):
        to = lax.rem(x + i + 1, 4)
        return remote(
            sc.at[lax.rem(j, 2), to], rc.at[j, :, x], c_s.at[j, 7 + i], c_r.at[j, 7 + i], xp[i]
        )

    def c_xown(j):
        return pltpu.make_async_copy(sc.at[lax.rem(j, 2), x], rc.at[j, :, x], c_s.at[j, 15])

    tail = pl.ds(MAIN, 128)

    def planes(part):
        return pl.ds(0, 1) if part == 0 else pl.ds(1, 3)

    def s_z(part, i):
        to = cp if i == 3 else zp[i]
        n = part * 7 + i
        return remote(
            yt.at[planes(part), :, tail], zs.at[planes(part), mine],
            c_s.at[NC, n], c_r.at[NC, n], to,
        )

    def s_own(part):
        return pltpu.make_async_copy(
            yt.at[planes(part), :, tail], zs.at[planes(part), mine], c_s.at[NC, 14 + part]
        )

    def s_c(part, i):
        n = part * 7 + 4 + i
        piece = zs.at[planes(part), src_rows(lax.rem(z + 3 - i, 4), c)]
        return remote(piece, piece, c_s.at[NC, n], c_r.at[NC, n], cp)

    def s_x(i):
        to = lax.rem(x + i + 1, 4)
        return remote(sss.at[to], rsd.at[:, x], c_s.at[NC + 1, i], c_r.at[NC + 1, i], xp[i])

    def s_xown():
        return pltpu.make_async_copy(sss.at[x], rsd.at[:, x], c_s.at[NC + 1, 14])

    def picks(i):
        row, lane = iota((8, 128), 0), iota((8, 128), 1)
        sel = jnp.where((lane == 64 + row * 8 + z * 2 + c) & (row < 4), 1.0, 0.0).astype(BF)
        slot = dot(sel, zs[i], 1, 1)
        r, t = iota((160, 1024), 0), iota((160, 1024), 1)
        key = jnp.where(
            lax.shift_right_logical(t, 7) == (r & 7), lax.shift_right_logical(r, 3), -5
        ).astype(F32)
        for xx in range(4):
            one = jnp.where(slot[xx : xx + 1, :] == key, 1.0, 0.0).astype(BF)
            sb[i, xx * 160 : (xx + 1) * 160, :] = one

    def g_core():
        there = pl.ds(pl.multiple_of((1 - c) * 256, 256), 256)
        return remote(s1.at[there], cb, g_s.at[0], g_r.at[0], cp)

    def g_z(i):
        to = lax.rem(z + i + 1, 4)
        rows = pl.ds(pl.multiple_of(c * 256 + to * 64, 64), 64)
        return remote(s1.at[rows], zb_.at[i], g_s.at[1 + i], g_r.at[1 + i], zp[i])

    def g_x(i):
        to = lax.rem(x + i + 1, 4)
        rows = pl.ds(pl.multiple_of(to * 16, 16), 16)
        return remote(p1.at[rows], xb_.at[i], g_s.at[4 + i], g_r.at[4 + i], xp[i])

    def h_x(i):
        rows = pl.ds(pl.multiple_of(x * 16, 16), 16)
        return remote(xg.at[rows], xg.at[rows], g_s.at[7 + i], g_r.at[7 + i], xp[i])

    at_z = pl.ds(pl.multiple_of(c * 256 + z * 64, 64), 64)

    def h_z(i):
        return remote(xg, total.at[at_z], g_s.at[10 + i], g_r.at[10 + i], zp[i])

    def h_own():
        return pltpu.make_async_copy(xg, total.at[at_z], g_s.at[14])

    def h_core():
        half = total.at[pl.ds(pl.multiple_of(c * 256, 256), 256)]
        return remote(half, half, g_s.at[13], g_r.at[13], cp)

    def hidden(b):
        return hid[pl.ds(b * 4, 4)].reshape(640, FF)

    def put(slot, k):
        return pltpu.make_async_copy(stg.at[slot], dg.at[:, cols_of(k)], ls.at[slot])

    def put_tail():
        return pltpu.make_async_copy(stl, dg.at[:, pl.ds(MAIN, 64)], ls.at[2])

    def work(slot, k):
        stg[slot] = dot(hgt[...], rbuf[slot], 1, 0).astype(BF)
        put(slot, k).start()

        @pl.loop(0, 4)
        def _(b):
            rb = pl.ds(pl.multiple_of(b * 640, 640), 640)
            g = dot(hidden(b), w[:, cols_of(k)], 1, 0)
            prod = g * rbuf[slot, rb, :].astype(F32)
            acc[rb, :] += prod[:, 0:128] + prod[:, 128:256]

    for i in range(4):
        s_z(0, i).start()
    s_own(0).start()
    for i in range(2):
        tok(0, i).start()

    def gate_hidden(_):
        s_xown().wait()
        for i in range(3):
            s_x(i).wait_recv()
        rows = rsd[...].reshape(ROWS, 128)
        sel = jnp.where(iota((8, 128), 1) == 96 + e, 1.0, 0.0).astype(BF)
        gate = dot(sel, rows, 1, 1)[0:1, :]

        @pl.loop(0, FF // 16)
        def _(b):
            rb = pl.ds(pl.multiple_of(b * 16, 16), 16)
            hgt[rb, :] = (hgt[rb, :].astype(F32) * gate).astype(BF)

        stl[...] = dot(hgt[...], rows, 1, 0)[:, 0:64].astype(BF)
        put_tail().start()
        @pl.loop(0, 4)
        def _(b):
            rb = pl.ds(pl.multiple_of(b * 640, 640), 640)
            g = dot(hidden(b), w[:, MAIN:D], 1, 0)
            part = rsd[b].reshape(640, 128)[:, 0:64].astype(F32)
            acc[rb, :] = jnp.concatenate([g * part, jnp.zeros((640, 64), F32)], axis=1)

    def tail_core(_):
        for i in range(3):
            s_z(1, i).wait_recv()
            s_c(1, i).start()

    def a_core(k):
        for i in range(3):
            a_z(k, i).wait_recv()
            a_c(k, i).start()

    def a_work(k):
        for i in range(2):
            a_f(k, i).wait_recv()
        fetch = pltpu.make_async_copy(ra.at[k], rbuf.at[0], ls.at[3])
        fetch.start()

        @pl.when(k > 0)
        def _():
            put(0, k - 1).wait()

        fetch.wait()
        work(0, k)

    def send_sections(_):
        for i in range(3):
            sections(i).start()
        own_section().start()

    def attn_part(_):
        @pl.loop(0, 4)
        def _(i):
            got = dot(yt[i, :, 0:D], pw[...], 1, 0).astype(BF)
            ms[lax.rem(i + 3, 4)] = got

        for i in range(3):
            back(i).start()
        mr[y] = ms[3]

    def known_part(_):
        for i in range(2):
            tok_f(1, i).wait_recv()
        own_section().wait()
        for i in range(3):
            sections(i).wait_recv()
        unit = eye(SEC)
        for i in range(4):
            aot[:, i * TOK : (i + 1) * TOK] = dot(unit, aos[i], 1, 1).astype(BF)

        @pl.loop(0, MAIN // CH)
        def _(k):
            block = yt[:, :, cols_of(k)].reshape(4 * TOK, CH)
            s1[:, cols_of(k)] = dot(aot[...], block, 1, 0).astype(BF)

        last = yt[:, :, MAIN:DP].reshape(4 * TOK, 128)
        s1[:, MAIN:D] = dot(aot[...], last, 1, 0)[:, 0:64].astype(BF)
        g_core().start()

    def tail_pick(_):
        s_own(1).wait()
        s_z(1, 3).wait_recv()
        for i in range(3):
            s_c(1, i).wait_recv()

        @pl.loop(1, 4)
        def _(i):
            picks(i)

        @pl.loop(0, 4)
        def _(i):
            got = dot(sb[i], zs[i], 1, 0).astype(BF)
            for xx in range(4):
                sss[xx, lax.rem(y + i, 4)] = got[xx * 160 : (xx + 1) * 160]

        for i in range(3):
            s_x(i).start()
        s_xown().start()

    def a_send_z(k):
        for i in range(4):
            a_z(k, i).start()
        a_own(k).start()

    def tail_z(_):
        for i in range(2):
            tok_f(0, i).wait_recv()
        for i in range(4):
            s_z(1, i).start()
        s_own(1).start()

    def tok_c_ring(_):
        for i in range(2):
            tok(0, i).wait_recv()
            tok_f(0, i).start()

    def tok_a_send(_):
        for i in range(2):
            tok(1, i).start()

    def y_send(k):
        a_xown(k).wait()
        for i in range(3):
            a_x(k, i).wait_recv()
        for i in range(2):
            a_y(k, i).start()

    def c_work(j):
        c_xown(j).wait()
        for i in range(3):
            c_x(j, i).wait_recv()
        fetches = [
            pltpu.make_async_copy(
                rc.at[j, yy, xx], rbuf.at[1, pl.ds(yy * 640 + xx * 160, 160)],
                ls.at[16 + yy * 4 + xx],
            )
            for yy in range(4) for xx in range(4)
        ]
        for f in fetches:
            f.start()

        @pl.when(j > 0)
        def _():
            put(1, NA + j - 1).wait()

        for f in fetches:
            f.wait()
        work(1, NA + j)

    def c_core(j):
        for i in range(3):
            c_z(j, i).wait_recv()
            c_c(j, i).start()

    def sum_core(_):
        g_core().wait()

        @pl.loop(0, 4)
        def _(b):
            here = pl.ds(pl.multiple_of(c * 256 + b * 64, 64), 64)
            there = pl.ds(pl.multiple_of(b * 64, 64), 64)
            s1[here, :] = (s1[here, :].astype(F32) + cb[there, :].astype(F32)).astype(BF)

        for i in range(3):
            g_z(i).start()

    def pack_hidden(_):
        @pl.loop(0, CAP // 2)
        def _(b):
            load_hid(b).wait()
            two = [
                dot(eye(TOK), hp[lax.rem(b, 2), h], 1, 1).reshape(16, 8, FF) for h in range(2)
            ]
            rows = pl.ds(pl.multiple_of(b * 16, 16), 16)
            hid[:, rows, :] = jnp.concatenate(two, axis=1).astype(BF)

            @pl.when(b < CAP // 2 - 2)
            def _():
                load_hid(b + 2).start()

        unit = eye(FF)

        @pl.loop(0, 4)
        def _(b):
            rb = pl.ds(pl.multiple_of(b * 640, 640), 640)
            hgt[:, rb] = dot(unit, hidden(b), 1, 1).astype(BF)

        loads[3].wait()
        loads[4].wait()
        loads[5].wait()
        rpo[...] = dot(rw[...], pw[...], 1, 0).astype(BF)
        for i in range(3):
            rp(i).start()
        rpt[y] = rpo[...]

    def c_pick(j):
        c_own(j).wait()
        c_z(j, 3).wait_recv()
        for i in range(3):
            c_c(j, i).wait_recv()

        @pl.when(j >= 2)
        def _():
            for i in range(3):
                c_x(j - 2, i).wait_send()

        @pl.loop(0, 4)
        def _(i):
            got = dot(sb[i], zc[j, i], 1, 0).astype(BF)
            for xx in range(4):
                sc[lax.rem(j, 2), xx, lax.rem(y + i, 4)] = got[xx * 160 : (xx + 1) * 160]

        for i in range(3):
            c_x(j, i).start()
        c_xown(j).start()

    def give_z(_):
        for i in range(3):
            h_x(i).wait_recv()
        for i in range(3):
            h_z(i).start()
        h_own().start()

    def give_core(_):
        for i in range(3):
            h_z(i).wait_recv()
        h_own().wait()
        h_core().start()

    def y_ring(k):
        for i in range(2):
            a_y(k, i).wait_recv()
            a_f(k, i).start()

    def sum_x(_):
        for i in range(3):
            g_x(i).wait_recv()
        rows = pl.ds(pl.multiple_of(x * 16, 16), 16)
        add = p1[rows, :].astype(F32) + xb_[0].astype(F32)
        xg[rows, :] = (add + (xb_[1].astype(F32) + xb_[2].astype(F32))).astype(BF)
        for i in range(3):
            h_x(i).start()

    def c_send_z(j):
        for i in range(4):
            c_z(j, i).start()
        c_own(j).start()

    def sum_z(_):
        for i in range(3):
            g_z(i).wait_recv()
        add = s1[at_z, :].astype(F32) + zb_[0].astype(F32)
        p1[...] = (add + (zb_[1].astype(F32) + zb_[2].astype(F32))).astype(BF)
        for i in range(3):
            g_x(i).start()

    def tok_a_ring(_):
        for i in range(2):
            tok(1, i).wait_recv()
            tok_f(1, i).start()

    def pick_own(_):
        s_own(0).wait()
        s_z(0, 3).wait_recv()
        for i in range(3):
            s_c(0, i).wait_recv()
        picks(0)

    def tail_own_core(_):
        for i in range(3):
            s_z(0, i).wait_recv()
            s_c(0, i).start()

    def a_pick(k):
        a_own(k).wait()
        a_z(k, 3).wait_recv()
        for i in range(3):
            a_c(k, i).wait_recv()
        got = dot(sb[0], za[k], 1, 0).astype(BF)
        for xx in range(4):
            sa[k, xx] = got[xx * 160 : (xx + 1) * 160]
        for i in range(3):
            a_x(k, i).start()
        a_xown(k).start()

    parts = {
        "gate_hidden": gate_hidden,
        "tail_core": tail_core,
        "a_core": a_core,
        "a_work": a_work,
        "send_sections": send_sections,
        "attn_part": attn_part,
        "known_part": known_part,
        "tail_pick": tail_pick,
        "a_send_z": a_send_z,
        "tail_z": tail_z,
        "tok_c_ring": tok_c_ring,
        "tok_a_send": tok_a_send,
        "y_send": y_send,
        "c_work": c_work,
        "c_core": c_core,
        "sum_core": sum_core,
        "pack_hidden": pack_hidden,
        "c_pick": c_pick,
        "give_z": give_z,
        "give_core": give_core,
        "y_ring": y_ring,
        "sum_x": sum_x,
        "c_send_z": c_send_z,
        "sum_z": sum_z,
        "tok_a_ring": tok_a_ring,
        "pick_own": pick_own,
        "tail_own_core": tail_own_core,
        "a_pick": a_pick,
    }

    @pl.loop(0, STEPS)
    def _(t):
        for key, at in AT.items():
            due = t == at[0]
            number = jnp.int32(0)
            for step in at[1:]:
                due = due | (t == step)
                number = number + jnp.where(t >= step, 1, 0)

            @pl.when(due)
            def _(part=parts[key], number=number):
                part(number)

    exact = lax.Precision.HIGHEST
    at_slot = iota((160, 128), 1) == lax.shift_right_logical(iota((160, 128), 0), 3)
    fold = jnp.where((iota((8, 160), 1) & 7) == iota((8, 160), 0), 1.0, 0.0)
    for b in range(16):
        sums = jnp.sum(acc[b * 160 : (b + 1) * 160, :], axis=1, keepdims=True)
        vs[b // 4, b % 4] = dot(fold, jnp.where(at_slot, sums, 0.0), 1, 0, exact)

    def v_y(i):
        return remote(
            vs.at[lax.rem(y + i + 1, 4)], yr.at[i], t_s.at[i], t_r.at[i], yp[i]
        )

    def v_x(i):
        to = lax.rem(x + i + 1, 4)
        return remote(vs.at[0, to], xr.at[x], t_s.at[3 + i], t_r.at[3 + i], xp[i])

    def v_z(i):
        return remote(xr, zr.at[:, z], t_s.at[6 + i], t_r.at[6 + i], zp[i])

    def v_c():
        return remote(zr, cr.at[:, :, c], t_s.at[9], t_r.at[9], cp)

    def r_y(i):
        return remote(rr.at[0], rr.at[3 - i], t_s.at[10 + i], t_r.at[10 + i], yp[i])

    def q_c():
        return remote(q0, q1, t_s.at[13], t_r.at[13], cp)

    def q_z(i):
        return remote(q2.at[0], q2.at[1 + i], t_s.at[14 + i], t_r.at[14 + i], zp[i])

    def q_x(i):
        return remote(q3.at[0], q3.at[1 + i], t_s.at[17 + i], t_r.at[17 + i], xp[i])

    for i in range(3):
        v_y(i).start()
    for i in range(3):
        v_y(i).wait()
    vs[0] = vs[y] + yr[0] + yr[1] + yr[2]
    for i in range(3):
        v_x(i).start()
    xr[x] = vs[0, x]
    for i in range(3):
        v_x(i).wait()
    for i in range(3):
        v_z(i).start()
    zr[:, z] = xr[...]
    for i in range(3):
        v_z(i).wait()
    v_c().start()
    cr[:, :, c] = zr[...]
    v_c().wait()
    got = cr[...].reshape(NE, 8, 128)
    got = jnp.sum(jnp.where(iota((NE, 8, 128), 1) == z * 2 + c, got, 0.0), axis=1)
    grad = jnp.zeros((NE, TOK), F32)
    for s in range(CAP):
        grad = grad + jnp.where(pos == s, got[:, s : s + 1], 0.0)
    inner = jnp.sum(dense * grad, axis=0, keepdims=True)
    full = dense * (grad - inner)
    rrow = full.astype(BF)
    rr[0] = rrow
    for i in range(3):
        r_y(i).start()
    row = iota((NE, TOK), 0)
    for k in range(4):
        hit = ids[k : k + 1, :] == row
        lg[k : k + 1, :] = jnp.sum(jnp.where(hit, full, 0.0), axis=0, keepdims=True)
    for i in range(3):
        r_y(i).wait()
    q = jnp.zeros((NE, SEC), F32)
    for t in range(4):
        q = q + dot(rr[t], aos[t], 1, 0)
    q0[...] = q
    q_c().start()
    for i in range(3):
        rp(i).wait()
        back(i).wait()
    for t in range(4):
        more = dot(rrow, rpt[t], 0, 0)
        attn[:, t * SEC : (t + 1) * SEC] = (mr[t].astype(F32) + more).astype(BF)
    q_c().wait()
    q2[0] = q0[...] + q1[...]
    for i in range(3):
        q_z(i).start()
    for i in range(3):
        q_z(i).wait()
    q3[0] = (q2[0] + q2[1]) + (q2[2] + q2[3])
    for i in range(3):
        q_x(i).start()
    for i in range(3):
        q_x(i).wait()
    qt[...] = (q3[0] + q3[1]) + (q3[2] + q3[3])

    put(0, NA - 1).wait()
    put(1, NA + NC - 1).wait()
    put_tail().wait()
    h_core().wait()
    for i in range(2):
        for part in range(2):
            tok(part, i).wait_send()
            tok_f(part, i).wait_send()
    for i in range(3):
        sections(i).wait_send()
        g_z(i).wait_send()
        g_x(i).wait_send()
        h_x(i).wait_send()
        h_z(i).wait_send()
        s_x(i).wait_send()
    for part in range(2):
        for i in range(4):
            s_z(part, i).wait_send()
        for i in range(3):
            s_c(part, i).wait_send()

    @pl.loop(0, NA)
    def _(k):
        for i in range(4):
            a_z(k, i).wait_send()
        for i in range(3):
            a_c(k, i).wait_send()
            a_x(k, i).wait_send()
        for i in range(2):
            a_y(k, i).wait_send()
            a_f(k, i).wait_send()

    @pl.loop(0, NC)
    def _(j):
        for i in range(4):
            c_z(j, i).wait_send()
        for i in range(3):
            c_c(j, i).wait_send()

        @pl.when(j >= NC - 2)
        def _():
            for i in range(3):
                c_x(j, i).wait_send()


def local(
    out_grad, expert_ids, chosen_logits, router_weight, hidden_act, down_weight, attn_out, proj_weight
):
    vm = pl.BlockSpec(memory_space=pltpu.VMEM)
    hbm = pl.BlockSpec(memory_space=pl.ANY)
    sds = jax.ShapeDtypeStruct
    sem = pltpu.SemaphoreType.DMA
    v = pltpu.VMEM
    dg, total, _, _, attn, lg, qt = pl.pallas_call(
        kernel,
        out_shape=(
            sds((FF, D), BF), sds((SEC, D), BF), sds((NA, ROWS, CH), BF),
            sds((NC, 4, 4, 160, CH), BF), sds((TOK, HID), BF), sds((4, TOK), F32),
            sds((NE, SEC), F32),
        ),
        in_specs=[hbm] * 8,
        out_specs=(hbm, hbm, hbm, hbm, vm, vm, vm),
        scratch_shapes=[
            v((D, TOK), BF), v((4, TOK), jnp.int32), v((4, TOK), F32), v((D, SEC), BF),
            v((NE, D), BF), v((2, 2, FF, TOK), BF), v((4, TOK, DP), BF),
            v((NA, 1024, CH), BF), v((NC, 4, 1024, CH), BF), v((4, 1024, 128), BF),
            v((4, 640, 1024), BF), v((NA, 4, 160, CH), BF), v((2, 4, 4, 160, CH), BF),
            v((4, 4, 160, 128), BF), v((4, 4, 160, 128), BF), v((2, ROWS, CH), BF),
            v((FF, D), BF), v((16, 160, FF), BF), v((FF, ROWS), BF),
            v((ROWS, 128), F32), v((2, FF, CH), BF), v((FF, 64), BF),
            v((4, TOK, SEC), BF), v((SEC, SEC), BF), v((4, TOK, SEC), BF), v((4, TOK, SEC), BF),
            v((NE, SEC), BF), v((4, NE, SEC), BF), v((SEC, D), BF), v((256, D), BF),
            v((3, 64, D), BF), v((64, D), BF), v((3, 16, D), BF), v((64, D), BF),
            v((4, 4, 8, 128), F32), v((3, 4, 8, 128), F32), v((4, 8, 128), F32),
            v((4, 4, 8, 128), F32), v((4, 4, 2, 8, 128), F32), v((4, NE, TOK), BF),
            v((NE, SEC), F32), v((NE, SEC), F32), v((4, NE, SEC), F32), v((4, NE, SEC), F32),
            sem((NA, 16)), sem((NA, 16)), sem((NC + 2, 16)), sem((NC + 2, 16)),
            sem((17,)), sem((17,)), sem((15,)), sem((15,)), sem((20,)), sem((20,)), sem((32,)),
        ],
        compiler_params=pltpu.CompilerParams(
            collective_id=0, has_side_effects=True, vmem_limit_bytes=62 * 2**20
        ),
        cost_estimate=pl.CostEstimate(
            flops=50 * 10**9, bytes_accessed=400 * 10**6, transcendentals=0
        ),
        name="layer_backward",
    )(
        out_grad.T, expert_ids.T, chosen_logits.T, attn_out, proj_weight.T, router_weight.T,
        jnp.transpose(hidden_act[0], (1, 2, 0)), down_weight[0],
    )
    more = dot(qt.astype(BF), router_weight, 0, 1)
    proj_grad = (total.astype(F32) + more).astype(BF)
    return attn, proj_grad, dg[None], lg.T


def solution(mesh):
    return jax.shard_map(
        local,
        mesh=mesh,
        in_specs=(
            P(("dp", "expert"), None),
            P(("dp", "expert"), None),
            P(("dp", "expert"), None),
            P(),
            P("expert", None, None, "dp"),
            P("expert", "dp", None),
            P(("dp", "expert"), None),
            P("dp", None),
        ),
        out_specs=(
            P(("dp", "expert"), None),
            P("dp", None),
            P("expert", "dp", None),
            P(("dp", "expert"), None),
        ),
        check_vma=False,
    )
```

```python
import functools

import jax
import jax.numpy as jnp
from jax import lax
from jax.experimental import pallas as pl
from jax.experimental.pallas import tpu as pltpu
from jax.sharding import PartitionSpec as P

MESH = pl.DeviceIdType.MESH
BF = jnp.bfloat16
F32 = jnp.float32
D = 2880
DP = 2944
MAIN = 2816
FF = 720
TOK = 128
NE = 32
CAP = 20
SEC = 512
HID = 2048
CH = 256
NA = 8
NC = 3
CB = NA * CH
STEPS = 29
AT = {
    "a_send_z": (0, 1, 2, 3, 5, 6, 8, 9),
    "pick_own": (3,),
    "attn_part": (17,),
    "tok_a_send": (1,),
    "sum_x": (24,),
    "c_core": (15, 19, 23),
    "pack_hidden": (1,),
    "tok_c_ring": (1,),
    "send_sections": (5,),
    "c_send_z": (7, 15, 19),
    "y_send": (6, 7, 10, 12, 13, 14, 19, 20),
    "sum_z": (21,),
    "a_pick": (3, 4, 6, 9, 10, 11, 17, 18),
    "c_work": (21, 23, 28),
    "tail_pick": (14,),
    "sum_core": (15,),
    "tail_core": (11,),
    "c_pick": (18, 20, 24),
    "tail_z": (6,),
    "tok_a_ring": (5,),
    "tail_own_core": (1,),
    "a_core": (1, 2, 4, 5, 7, 8, 15, 16),
    "gate_hidden": (19,),
    "known_part": (11,),
    "y_ring": (11, 14, 16, 18, 19, 20, 23, 25),
    "give_z": (25,),
    "a_work": (20, 21, 22, 24, 25, 26, 27, 28),
    "give_core": (28,),
}
ROWS = 2560


def dot(a, b, ca, cb, precision=None):
    return lax.dot_general(
        a, b, (((ca,), (cb,)), ((), ())), preferred_element_type=F32, precision=precision
    )


def iota(shape, dim):
    return lax.broadcasted_iota(jnp.int32, shape, dim)


def place():
    y = lax.axis_index("dp")
    e = lax.axis_index("expert")
    x = lax.div(e, 8)
    z = lax.rem(lax.div(e, 2), 4)
    c = lax.rem(e, 2)
    return y, x, z, c


def dev(y, x, z, c):
    return (lax.rem(y, 4), lax.rem(x, 4) * 8 + lax.rem(z, 4) * 2 + c)


def remote(src, dst, ss, rs, to):
    return pltpu.make_async_remote_copy(
        src_ref=src, dst_ref=dst, send_sem=ss, recv_sem=rs, device_id=to, device_id_type=MESH
    )


def greet(peers):
    bar = pltpu.get_barrier_semaphore()
    for p in peers:
        pl.semaphore_signal(bar, inc=1, device_id=p, device_id_type=MESH)
    pl.semaphore_wait(bar, len(peers))


def dense_gates(ids, logits):
    row = iota((NE, TOK), 0)
    w = jnp.exp(logits[...])
    gates = w / jnp.sum(w, axis=0, keepdims=True)
    chosen = jnp.zeros((NE, TOK), F32)
    dense = jnp.zeros((NE, TOK), F32)
    for k in range(4):
        hit = ids[k : k + 1, :] == row
        chosen = chosen + jnp.where(hit, 1.0, 0.0)
        dense = dense + jnp.where(hit, gates[k : k + 1, :], 0.0)
    upper = jnp.where(iota((TOK, TOK), 0) < iota((TOK, TOK), 1), 1.0, 0.0).astype(BF)
    count = dot(chosen.astype(BF), upper, 1, 0)
    return dense, jnp.where(chosen > 0.0, count, -1.0)


def eye(n):
    return jnp.where(iota((n, n), 0) == iota((n, n), 1), 1.0, 0.0).astype(BF)


def four(ref):
    part = [ref[i].astype(F32) for i in range(4)]
    return ((part[0] + part[1]) + (part[2] + part[3])).astype(BF)


def kernel(
    og_h, ids_h, log_h, ao, pw_h, rw_h, hid_h, w_h,
    dg, total, ra, rc, attn, lg, qt,
    og, ids, logits, pw, rw, hp, yt, za, zc, zs, sb, sa, sc, sss, rsd, rbuf, w, hid, hgt, acc,
    stg, stl, aos, aot, ms, mr, rpo, rpt, s1, cb, zb_, p1, xb_, xg,
    vs, yr, xr, cr, rr, q0, q3,
    a_s, a_r, c_s, c_r, k_s, k_r, g_s, g_r, t_s, t_r, ls,
):
    y, x, z, c = place()
    e = x * 8 + z * 2 + c
    zp = [dev(y, x, z + i, c) for i in (1, 2, 3)]
    xp = [dev(y, x + i, z, c) for i in (1, 2, 3)]
    yp = [dev(y + i, x, z, c) for i in (1, 2, 3)]
    cp = dev(y, x, z, 1 - c)
    yxp = [dev(y + n // 4, x + n % 4, z, c) for n in range(16)]
    zcp = [dev(y, x, z + m // 2, lax.rem(c + m % 2, 2)) for m in range(8)]
    loads = [
        pltpu.make_async_copy(a, b, ls.at[5 + n])
        for n, (a, b) in enumerate(
            [(og_h, og), (ids_h, ids), (log_h, logits), (rw_h, rw), (pw_h, pw), (w_h, w)]
        )
    ]

    def load_hid(b):
        return pltpu.make_async_copy(
            hid_h.at[pl.ds(b * 2, 2)], hp.at[lax.rem(b, 2)], ls.at[11 + lax.rem(b, 2)]
        )

    for l in loads:
        l.start()
    load_hid(0).start()
    load_hid(1).start()
    greet(yxp[1:] + zcp[1:])
    for l in loads[:3]:
        l.wait()
    dense, pos = dense_gates(ids, logits)
    side = [og[MAIN:D, :], pos.astype(BF), dense.astype(BF)]
    yt[0, :, MAIN:DP] = dot(eye(TOK), jnp.concatenate(side, axis=0), 1, 1).astype(BF)

    @pl.loop(NA, NA + NC)
    def _(k):
        rows = pl.ds(pl.multiple_of(k * CH, CH), CH)
        yt[0, :, rows] = dot(eye(TOK), og[rows, :], 1, 1).astype(BF)

    def src_rows(zz, cc):
        return pl.ds(pl.multiple_of((zz * 2 + cc) * TOK, TOK), TOK)

    mine = src_rows(z, c)

    def cols_of(k):
        return pl.ds(pl.multiple_of(k * CH, CH), CH)

    def tok(part, i):
        cols = pl.ds(CB, DP - CB) if part == 0 else pl.ds(0, CB)
        n = part * 4 + i
        return remote(
            yt.at[0, :, cols], yt.at[3 if i == 0 else 1, :, cols], k_s.at[n], k_r.at[n], yp[2 * i]
        )

    def tok_f(part, i):
        cols = pl.ds(CB, DP - CB) if part == 0 else pl.ds(0, CB)
        n = part * 4 + 2 + i
        rows = pl.ds(64 * i, 64)
        return remote(
            yt.at[3 if i == 0 else 1, rows, cols], yt.at[2, rows, cols],
            k_s.at[n], k_r.at[n], yp[2 * i],
        )

    def sections(i):
        to = lax.rem(y + i + 1, 4)
        cols = pl.ds(pl.multiple_of(to * SEC, SEC), SEC)
        return remote(ao.at[:, cols], aos.at[3 - i], k_s.at[8 + i], k_r.at[8 + i], yp[i])

    def own_section():
        cols = pl.ds(pl.multiple_of(y * SEC, SEC), SEC)
        return pltpu.make_async_copy(ao.at[:, cols], aos.at[0], ls.at[13])

    def rp(i):
        return remote(rpo, rpt.at[y], k_s.at[11 + i], k_r.at[11 + i], yp[i])

    def back(i):
        return remote(ms.at[i], mr.at[y], k_s.at[14 + i], k_r.at[14 + i], yp[i])

    def a_z(k, i):
        to = cp if i == 3 else zp[i]
        return remote(
            yt.at[0, :, cols_of(k)], za.at[k, mine], a_s.at[k, i], a_r.at[k, i], to
        )

    def a_own(k):
        return pltpu.make_async_copy(yt.at[0, :, cols_of(k)], za.at[k, mine], a_s.at[k, 14])

    def a_c(k, i):
        part = za.at[k, src_rows(lax.rem(z + 3 - i, 4), c)]
        return remote(part, part, a_s.at[k, 4 + i], a_r.at[k, 4 + i], cp)

    def x_rows(yy, xx):
        return pl.ds(pl.multiple_of(yy * 640 + xx * 160, 160), 160)

    def a_x(k, i):
        to = lax.rem(x + i + 1, 4)
        return remote(
            sa.at[k, to], ra.at[k, x_rows(y, x)], a_s.at[k, 7 + i], a_r.at[k, 7 + i], xp[i]
        )

    def a_xown(k):
        return pltpu.make_async_copy(sa.at[k, x], ra.at[k, x_rows(y, x)], a_s.at[k, 15])

    def a_y(k, i):
        part = ra.at[k, pl.ds(pl.multiple_of(y * 640, 640), 640)]
        return remote(part, part, a_s.at[k, 10 + i], a_r.at[k, 10 + i], yp[2 * i])

    def a_f(k, i):
        src = lax.rem(y + (3 if i == 0 else 1), 4)
        part = ra.at[k, pl.ds(pl.multiple_of(src * 640 + 320 * i, 320), 320)]
        return remote(part, part, a_s.at[k, 12 + i], a_r.at[k, 12 + i], yp[2 * i])

    def c_z(j, i):
        to = cp if i == 3 else zp[i]
        return remote(
            yt.at[:, :, cols_of(NA + j)], zc.at[j, :, mine], c_s.at[j, i], c_r.at[j, i], to
        )

    def c_own(j):
        return pltpu.make_async_copy(
            yt.at[:, :, cols_of(NA + j)], zc.at[j, :, mine], c_s.at[j, 14]
        )

    def c_c(j, i):
        part = zc.at[j, :, src_rows(lax.rem(z + 3 - i, 4), c)]
        return remote(part, part, c_s.at[j, 4 + i], c_r.at[j, 4 + i], cp)

    def c_x(j, i):
        to = lax.rem(x + i + 1, 4)
        return remote(
            sc.at[lax.rem(j, 2), to], rc.at[j, :, x], c_s.at[j, 7 + i], c_r.at[j, 7 + i], xp[i]
        )

    def c_xown(j):
        return pltpu.make_async_copy(sc.at[lax.rem(j, 2), x], rc.at[j, :, x], c_s.at[j, 15])

    tail = pl.ds(MAIN, 128)

    def planes(part):
        return pl.ds(0, 1) if part == 0 else pl.ds(1, 3)

    def s_z(part, i):
        to = cp if i == 3 else zp[i]
        n = part * 7 + i
        return remote(
            yt.at[planes(part), :, tail], zs.at[planes(part), mine],
            c_s.at[NC, n], c_r.at[NC, n], to,
        )

    def s_own(part):
        return pltpu.make_async_copy(
            yt.at[planes(part), :, tail], zs.at[planes(part), mine], c_s.at[NC, 14 + part]
        )

    def s_c(part, i):
        n = part * 7 + 4 + i
        piece = zs.at[planes(part), src_rows(lax.rem(z + 3 - i, 4), c)]
        return remote(piece, piece, c_s.at[NC, n], c_r.at[NC, n], cp)

    def s_x(i):
        to = lax.rem(x + i + 1, 4)
        return remote(sss.at[to], rsd.at[:, x], c_s.at[NC + 1, i], c_r.at[NC + 1, i], xp[i])

    def s_xown():
        return pltpu.make_async_copy(sss.at[x], rsd.at[:, x], c_s.at[NC + 1, 14])

    def picks(i):
        row, lane = iota((8, 128), 0), iota((8, 128), 1)
        sel = jnp.where((lane == 64 + row * 8 + z * 2 + c) & (row < 4), 1.0, 0.0).astype(BF)
        slot = dot(sel, zs[i], 1, 1)
        r, t = iota((160, 1024), 0), iota((160, 1024), 1)
        key = jnp.where(
            lax.shift_right_logical(t, 7) == (r & 7), lax.shift_right_logical(r, 3), -5
        ).astype(F32)
        for xx in range(4):
            one = jnp.where(slot[xx : xx + 1, :] == key, 1.0, 0.0).astype(BF)
            sb[i, xx * 160 : (xx + 1) * 160, :] = one

    def g_core():
        there = pl.ds(pl.multiple_of((1 - c) * 256, 256), 256)
        return remote(s1.at[there], cb, g_s.at[0], g_r.at[0], cp)

    def g_z(i):
        to = lax.rem(z + i + 1, 4)
        rows = pl.ds(pl.multiple_of(c * 256 + to * 64, 64), 64)
        return remote(s1.at[rows], zb_.at[i], g_s.at[1 + i], g_r.at[1 + i], zp[i])

    def g_x(i):
        to = lax.rem(x + i + 1, 4)
        rows = pl.ds(pl.multiple_of(to * 16, 16), 16)
        return remote(p1.at[rows], xb_.at[i], g_s.at[4 + i], g_r.at[4 + i], xp[i])

    def h_x(i):
        rows = pl.ds(pl.multiple_of(x * 16, 16), 16)
        return remote(xg.at[rows], xg.at[rows], g_s.at[7 + i], g_r.at[7 + i], xp[i])

    at_z = pl.ds(pl.multiple_of(c * 256 + z * 64, 64), 64)

    def h_z(i):
        return remote(xg, total.at[at_z], g_s.at[10 + i], g_r.at[10 + i], zp[i])

    def h_own():
        return pltpu.make_async_copy(xg, total.at[at_z], g_s.at[14])

    def h_core():
        half = total.at[pl.ds(pl.multiple_of(c * 256, 256), 256)]
        return remote(half, half, g_s.at[13], g_r.at[13], cp)

    def hidden(b):
        return hid[pl.ds(b * 4, 4)].reshape(640, FF)

    def put(slot, k):
        return pltpu.make_async_copy(stg.at[slot], dg.at[:, cols_of(k)], ls.at[slot])

    def put_tail():
        return pltpu.make_async_copy(stl, dg.at[:, pl.ds(MAIN, 64)], ls.at[2])

    def work(slot, k):
        stg[slot] = dot(hgt[...], rbuf[slot], 1, 0).astype(BF)
        put(slot, k).start()

        @pl.loop(0, 4)
        def _(b):
            rb = pl.ds(pl.multiple_of(b * 640, 640), 640)
            g = dot(hidden(b), w[:, cols_of(k)], 1, 0)
            prod = g * rbuf[slot, rb, :].astype(F32)
            acc[rb, :] += prod[:, 0:128] + prod[:, 128:256]

    for i in range(4):
        s_z(0, i).start()
    s_own(0).start()
    for i in range(2):
        tok(0, i).start()

    @pl.loop(0, NA)
    def _(k):
        rows = pl.ds(pl.multiple_of(k * CH, CH), CH)
        yt[0, :, rows] = dot(eye(TOK), og[rows, :], 1, 1).astype(BF)


    def a_send_z(k):
        for i in range(4):
            a_z(k, i).start()
        a_own(k).start()

    def pick_own(_):
        s_own(0).wait()
        s_z(0, 3).wait_recv()
        for i in range(3):
            s_c(0, i).wait_recv()
        picks(0)

    def attn_part(_):
        @pl.loop(0, 4)
        def _(i):
            got = dot(yt[i, :, 0:D], pw[...], 1, 0).astype(BF)
            ms[lax.rem(i + 3, 4)] = got

        for i in range(3):
            back(i).start()
        mr[y] = ms[3]

    def tok_a_send(_):
        for i in range(2):
            tok(1, i).start()

    def sum_x(_):
        for i in range(3):
            g_x(i).wait_recv()
        rows = pl.ds(pl.multiple_of(x * 16, 16), 16)
        add = p1[rows, :].astype(F32) + xb_[0].astype(F32)
        xg[rows, :] = (add + (xb_[1].astype(F32) + xb_[2].astype(F32))).astype(BF)
        for i in range(3):
            h_x(i).start()

    def c_core(j):
        for i in range(3):
            c_z(j, i).wait_recv()
            c_c(j, i).start()

    def pack_hidden(_):
        @pl.loop(0, CAP // 2)
        def _(b):
            load_hid(b).wait()
            two = [
                dot(eye(TOK), hp[lax.rem(b, 2), h], 1, 1).reshape(16, 8, FF) for h in range(2)
            ]
            rows = pl.ds(pl.multiple_of(b * 16, 16), 16)
            hid[:, rows, :] = jnp.concatenate(two, axis=1).astype(BF)

            @pl.when(b < CAP // 2 - 2)
            def _():
                load_hid(b + 2).start()

        unit = eye(FF)

        @pl.loop(0, 4)
        def _(b):
            rb = pl.ds(pl.multiple_of(b * 640, 640), 640)
            hgt[:, rb] = dot(unit, hidden(b), 1, 1).astype(BF)

        loads[3].wait()
        loads[4].wait()
        loads[5].wait()
        rpo[...] = dot(rw[...], pw[...], 1, 0).astype(BF)
        for i in range(3):
            rp(i).start()
        rpt[y] = rpo[...]

    def tok_c_ring(_):
        for i in range(2):
            tok(0, i).wait_recv()
            tok_f(0, i).start()

    def send_sections(_):
        for i in range(3):
            sections(i).start()
        own_section().start()

    def c_send_z(j):
        for i in range(4):
            c_z(j, i).start()
        c_own(j).start()

    def y_send(k):
        a_xown(k).wait()
        for i in range(3):
            a_x(k, i).wait_recv()
        for i in range(2):
            a_y(k, i).start()

    def sum_z(_):
        for i in range(3):
            g_z(i).wait_recv()
        add = s1[at_z, :].astype(F32) + zb_[0].astype(F32)
        p1[...] = (add + (zb_[1].astype(F32) + zb_[2].astype(F32))).astype(BF)
        for i in range(3):
            g_x(i).start()

    def a_pick(k):
        a_own(k).wait()
        a_z(k, 3).wait_recv()
        for i in range(3):
            a_c(k, i).wait_recv()
        got = dot(sb[0], za[k], 1, 0).astype(BF)
        for xx in range(4):
            sa[k, xx] = got[xx * 160 : (xx + 1) * 160]
        for i in range(3):
            a_x(k, i).start()
        a_xown(k).start()

    def c_work(j):
        c_xown(j).wait()
        for i in range(3):
            c_x(j, i).wait_recv()
        fetches = [
            pltpu.make_async_copy(
                rc.at[j, yy, xx], rbuf.at[1, pl.ds(yy * 640 + xx * 160, 160)],
                ls.at[16 + yy * 4 + xx],
            )
            for yy in range(4) for xx in range(4)
        ]
        for f in fetches:
            f.start()

        @pl.when(j > 0)
        def _():
            put(1, NA + j - 1).wait()

        for f in fetches:
            f.wait()
        work(1, NA + j)

    def tail_pick(_):
        s_own(1).wait()
        s_z(1, 3).wait_recv()
        for i in range(3):
            s_c(1, i).wait_recv()

        @pl.loop(1, 4)
        def _(i):
            picks(i)

        @pl.loop(0, 4)
        def _(i):
            got = dot(sb[i], zs[i], 1, 0).astype(BF)
            for xx in range(4):
                sss[xx, lax.rem(y + i, 4)] = got[xx * 160 : (xx + 1) * 160]

        for i in range(3):
            s_x(i).start()
        s_xown().start()

    def sum_core(_):
        g_core().wait()

        @pl.loop(0, 4)
        def _(b):
            here = pl.ds(pl.multiple_of(c * 256 + b * 64, 64), 64)
            there = pl.ds(pl.multiple_of(b * 64, 64), 64)
            s1[here, :] = (s1[here, :].astype(F32) + cb[there, :].astype(F32)).astype(BF)

        for i in range(3):
            g_z(i).start()

    def tail_core(_):
        for i in range(3):
            s_z(1, i).wait_recv()
            s_c(1, i).start()

    def c_pick(j):
        c_own(j).wait()
        c_z(j, 3).wait_recv()
        for i in range(3):
            c_c(j, i).wait_recv()

        @pl.when(j >= 2)
        def _():
            for i in range(3):
                c_x(j - 2, i).wait_send()

        @pl.loop(0, 4)
        def _(i):
            got = dot(sb[i], zc[j, i], 1, 0).astype(BF)
            for xx in range(4):
                sc[lax.rem(j, 2), xx, lax.rem(y + i, 4)] = got[xx * 160 : (xx + 1) * 160]

        for i in range(3):
            c_x(j, i).start()
        c_xown(j).start()

    def tail_z(_):
        for i in range(2):
            tok_f(0, i).wait_recv()
        for i in range(4):
            s_z(1, i).start()
        s_own(1).start()

    def tok_a_ring(_):
        for i in range(2):
            tok(1, i).wait_recv()
            tok_f(1, i).start()

    def tail_own_core(_):
        for i in range(3):
            s_z(0, i).wait_recv()
            s_c(0, i).start()

    def a_core(k):
        for i in range(3):
            a_z(k, i).wait_recv()
            a_c(k, i).start()

    def gate_hidden(_):
        s_xown().wait()
        for i in range(3):
            s_x(i).wait_recv()
        rows = rsd[...].reshape(ROWS, 128)
        sel = jnp.where(iota((8, 128), 1) == 96 + e, 1.0, 0.0).astype(BF)
        gate = dot(sel, rows, 1, 1)[0:1, :]

        @pl.loop(0, FF // 16)
        def _(b):
            rb = pl.ds(pl.multiple_of(b * 16, 16), 16)
            hgt[rb, :] = (hgt[rb, :].astype(F32) * gate).astype(BF)

        stl[...] = dot(hgt[...], rows, 1, 0)[:, 0:64].astype(BF)
        put_tail().start()
        @pl.loop(0, 4)
        def _(b):
            rb = pl.ds(pl.multiple_of(b * 640, 640), 640)
            g = dot(hidden(b), w[:, MAIN:D], 1, 0)
            part = rsd[b].reshape(640, 128)[:, 0:64].astype(F32)
            acc[rb, :] = jnp.concatenate([g * part, jnp.zeros((640, 64), F32)], axis=1)

    def known_part(_):
        for i in range(2):
            tok_f(1, i).wait_recv()
        own_section().wait()
        for i in range(3):
            sections(i).wait_recv()
        unit = eye(SEC)
        for i in range(4):
            aot[:, i * TOK : (i + 1) * TOK] = dot(unit, aos[i], 1, 1).astype(BF)

        @pl.loop(0, MAIN // CH)
        def _(k):
            block = yt[:, :, cols_of(k)].reshape(4 * TOK, CH)
            s1[:, cols_of(k)] = dot(aot[...], block, 1, 0).astype(BF)

        last = yt[:, :, MAIN:DP].reshape(4 * TOK, 128)
        s1[:, MAIN:D] = dot(aot[...], last, 1, 0)[:, 0:64].astype(BF)
        g_core().start()

    def y_ring(k):
        for i in range(2):
            a_y(k, i).wait_recv()
            a_f(k, i).start()

    def give_z(_):
        for i in range(3):
            h_x(i).wait_recv()
        for i in range(3):
            h_z(i).start()
        h_own().start()

    def a_work(k):
        for i in range(2):
            a_f(k, i).wait_recv()
        fetch = pltpu.make_async_copy(ra.at[k], rbuf.at[0], ls.at[3])
        fetch.start()

        @pl.when(k > 0)
        def _():
            put(0, k - 1).wait()

        fetch.wait()
        work(0, k)

    def give_core(_):
        for i in range(3):
            h_z(i).wait_recv()
        h_own().wait()
        h_core().start()

    parts = {
        "a_send_z": a_send_z,
        "pick_own": pick_own,
        "attn_part": attn_part,
        "tok_a_send": tok_a_send,
        "sum_x": sum_x,
        "c_core": c_core,
        "pack_hidden": pack_hidden,
        "tok_c_ring": tok_c_ring,
        "send_sections": send_sections,
        "c_send_z": c_send_z,
        "y_send": y_send,
        "sum_z": sum_z,
        "a_pick": a_pick,
        "c_work": c_work,
        "tail_pick": tail_pick,
        "sum_core": sum_core,
        "tail_core": tail_core,
        "c_pick": c_pick,
        "tail_z": tail_z,
        "tok_a_ring": tok_a_ring,
        "tail_own_core": tail_own_core,
        "a_core": a_core,
        "gate_hidden": gate_hidden,
        "known_part": known_part,
        "y_ring": y_ring,
        "give_z": give_z,
        "a_work": a_work,
        "give_core": give_core,
    }

    @pl.loop(0, STEPS)
    def _(t):
        for key, at in AT.items():
            due = t == at[0]
            number = jnp.int32(0)
            for step in at[1:]:
                due = due | (t == step)
                number = number + jnp.where(t >= step, 1, 0)

            @pl.when(due)
            def _(part=parts[key], number=number):
                part(number)

    at_slot = iota((4, CAP, 8, 128), 3) == iota((4, CAP, 8, 128), 1)
    for b in range(4):
        block = acc[b * 640 : (b + 1) * 640, :].reshape(4, CAP, 8, 128)
        sums = jnp.sum(block, axis=3, keepdims=True)
        vs[b] = jnp.sum(jnp.where(at_slot, sums, 0.0), axis=1)

    def v_yx(n):
        block = vs.at[lax.rem(y + n // 4, 4), lax.rem(x + n % 4, 4)]
        return remote(block, yr.at[n], t_s.at[n], t_r.at[n], yxp[n])

    def v_zc(m):
        return remote(xr, cr.at[:, z, c], t_s.at[16 + m], t_r.at[16 + m], zcp[m])

    def r_y(i):
        return remote(rr.at[0], rr.at[3 - i], t_s.at[24 + i], t_r.at[24 + i], yp[i])

    def q_zc(m):
        return remote(q0.at[0], q0.at[m], t_s.at[27 + m], t_r.at[27 + m], zcp[m])

    def q_x(i):
        return remote(q3.at[0], q3.at[1 + i], t_s.at[35 + i], t_r.at[35 + i], xp[i])

    for n in range(1, 16):
        v_yx(n).start()
    yr[0] = vs[y, x]
    for n in range(1, 16):
        v_yx(n).wait()
    for n in range(4):
        xr[lax.rem(x + 4 - n, 4)] = (yr[n] + yr[4 + n]) + (yr[8 + n] + yr[12 + n])
    for m in range(1, 8):
        v_zc(m).start()
    cr[:, z, c] = xr[...]
    for m in range(1, 8):
        v_zc(m).wait()
    got = cr[...].reshape(NE, 8, 128)
    got = jnp.sum(jnp.where(iota((NE, 8, 128), 1) == z * 2 + c, got, 0.0), axis=1)
    grad = jnp.zeros((NE, TOK), F32)
    for s in range(CAP):
        grad = grad + jnp.where(pos == s, got[:, s : s + 1], 0.0)
    inner = jnp.sum(dense * grad, axis=0, keepdims=True)
    full = dense * (grad - inner)
    rrow = full.astype(BF)
    rr[0] = rrow
    for i in range(3):
        r_y(i).start()
    row = iota((NE, TOK), 0)
    for k in range(4):
        hit = ids[k : k + 1, :] == row
        lg[k : k + 1, :] = jnp.sum(jnp.where(hit, full, 0.0), axis=0, keepdims=True)
    for i in range(3):
        r_y(i).wait()
    q = jnp.zeros((NE, SEC), F32)
    for t in range(4):
        q = q + dot(rr[t], aos[t], 1, 0)
    q0[0] = q.astype(BF)
    for m in range(1, 8):
        q_zc(m).start()
    for i in range(3):
        rp(i).wait()
        back(i).wait()
    for t in range(4):
        more = dot(rrow, rpt[t], 0, 0)
        attn[:, t * SEC : (t + 1) * SEC] = (mr[t].astype(F32) + more).astype(BF)
    for m in range(1, 8):
        q_zc(m).wait()
    eight = [q0[m].astype(F32) for m in range(8)]
    while len(eight) > 1:
        eight = [eight[m] + eight[m + 1] for m in range(0, len(eight), 2)]
    q3[0] = eight[0].astype(BF)
    for i in range(3):
        q_x(i).start()
    for i in range(3):
        q_x(i).wait()
    qt[...] = four(q3)

    put(0, NA - 1).wait()
    put(1, NA + NC - 1).wait()
    put_tail().wait()
    h_core().wait()
    for i in range(2):
        for part in range(2):
            tok(part, i).wait_send()
            tok_f(part, i).wait_send()
    for i in range(3):
        sections(i).wait_send()
        g_z(i).wait_send()
        g_x(i).wait_send()
        h_x(i).wait_send()
        h_z(i).wait_send()
        s_x(i).wait_send()
    for part in range(2):
        for i in range(4):
            s_z(part, i).wait_send()
        for i in range(3):
            s_c(part, i).wait_send()

    @pl.loop(0, NA)
    def _(k):
        for i in range(4):
            a_z(k, i).wait_send()
        for i in range(3):
            a_c(k, i).wait_send()
            a_x(k, i).wait_send()
        for i in range(2):
            a_y(k, i).wait_send()
            a_f(k, i).wait_send()

    @pl.loop(0, NC)
    def _(j):
        for i in range(4):
            c_z(j, i).wait_send()
        for i in range(3):
            c_c(j, i).wait_send()

        @pl.when(j >= NC - 2)
        def _():
            for i in range(3):
                c_x(j, i).wait_send()


def local(
    out_grad, expert_ids, chosen_logits, router_weight, hidden_act, down_weight, attn_out, proj_weight
):
    vm = pl.BlockSpec(memory_space=pltpu.VMEM)
    hbm = pl.BlockSpec(memory_space=pl.ANY)
    sds = jax.ShapeDtypeStruct
    sem = pltpu.SemaphoreType.DMA
    v = pltpu.VMEM
    dg, total, _, _, attn, lg, qt = pl.pallas_call(
        kernel,
        out_shape=(
            sds((FF, D), BF), sds((SEC, D), BF), sds((NA, ROWS, CH), BF),
            sds((NC, 4, 4, 160, CH), BF), sds((TOK, HID), BF), sds((4, TOK), F32),
            sds((NE, SEC), BF),
        ),
        in_specs=[hbm] * 8,
        out_specs=(hbm, hbm, hbm, hbm, vm, vm, vm),
        scratch_shapes=[
            v((D, TOK), BF), v((4, TOK), jnp.int32), v((4, TOK), F32), v((D, SEC), BF),
            v((NE, D), BF), v((2, 2, FF, TOK), BF), v((4, TOK, DP), BF),
            v((NA, 1024, CH), BF), v((NC, 4, 1024, CH), BF), v((4, 1024, 128), BF),
            v((4, 640, 1024), BF), v((NA, 4, 160, CH), BF), v((2, 4, 4, 160, CH), BF),
            v((4, 4, 160, 128), BF), v((4, 4, 160, 128), BF), v((2, ROWS, CH), BF),
            v((FF, D), BF), v((16, 160, FF), BF), v((FF, ROWS), BF),
            v((ROWS, 128), F32), v((2, FF, CH), BF), v((FF, 64), BF),
            v((4, TOK, SEC), BF), v((SEC, SEC), BF), v((4, TOK, SEC), BF), v((4, TOK, SEC), BF),
            v((NE, SEC), BF), v((4, NE, SEC), BF), v((SEC, D), BF), v((256, D), BF),
            v((3, 64, D), BF), v((64, D), BF), v((3, 16, D), BF), v((64, D), BF),
            v((4, 4, 8, 128), F32), v((16, 8, 128), F32), v((4, 8, 128), F32),
            v((4, 4, 2, 8, 128), F32), v((4, NE, TOK), BF),
            v((8, NE, SEC), BF), v((4, NE, SEC), BF),
            sem((NA, 16)), sem((NA, 16)), sem((NC + 2, 16)), sem((NC + 2, 16)),
            sem((17,)), sem((17,)), sem((15,)), sem((15,)), sem((40,)), sem((40,)), sem((32,)),
        ],
        compiler_params=pltpu.CompilerParams(
            collective_id=0, has_side_effects=True, vmem_limit_bytes=62 * 2**20
        ),
        cost_estimate=pl.CostEstimate(
            flops=50 * 10**9, bytes_accessed=400 * 10**6, transcendentals=0
        ),
        name="layer_backward",
    )(
        out_grad.T, expert_ids.T, chosen_logits.T, attn_out, proj_weight.T, router_weight.T,
        jnp.transpose(hidden_act[0], (1, 2, 0)), down_weight[0],
    )
    more = dot(qt, router_weight, 0, 1)
    proj_grad = (total.astype(F32) + more).astype(BF)
    return attn, proj_grad, dg[None], lg.T


def solution(mesh):
    return jax.shard_map(
        local,
        mesh=mesh,
        in_specs=(
            P(("dp", "expert"), None),
            P(("dp", "expert"), None),
            P(("dp", "expert"), None),
            P(),
            P("expert", None, None, "dp"),
            P("expert", "dp", None),
            P(("dp", "expert"), None),
            P("dp", None),
        ),
        out_specs=(
            P(("dp", "expert"), None),
            P("dp", None),
            P("expert", "dp", None),
            P(("dp", "expert"), None),
        ),
        check_vma=False,
    )
```

```python
import functools

import jax
import jax.numpy as jnp
from jax import lax
from jax.experimental import pallas as pl
from jax.experimental.pallas import tpu as pltpu
from jax.sharding import PartitionSpec as P

MESH = pl.DeviceIdType.MESH
BF = jnp.bfloat16
F32 = jnp.float32
D = 2880
DP = 2944
MAIN = 2816
FF = 720
TOK = 128
NE = 32
CAP = 20
SEC = 512
HID = 2048
CH = 256
NA = 8
NC = 3
CB = NA * CH
STEPS = 29
AT = {
    "a_send_z": (0, 1, 2, 3, 5, 6, 8, 9),
    "pick_own": (3,),
    "attn_part": (17,),
    "tok_a_send": (1,),
    "sum_x": (24,),
    "c_core": (15, 19, 23),
    "pack_hidden": (1,),
    "tok_c_ring": (1,),
    "send_sections": (5,),
    "c_send_z": (7, 15, 19),
    "y_send": (6, 7, 10, 12, 13, 14, 19, 20),
    "sum_z": (21,),
    "a_pick": (3, 4, 6, 9, 10, 11, 17, 18),
    "c_work": (21, 23, 28),
    "tail_pick": (14,),
    "sum_core": (15,),
    "tail_core": (11,),
    "c_pick": (18, 20, 24),
    "tail_z": (6,),
    "tok_a_ring": (5,),
    "tail_own_core": (1,),
    "a_core": (1, 2, 4, 5, 7, 8, 15, 16),
    "gate_hidden": (19,),
    "known_part": (11,),
    "y_ring": (11, 14, 16, 18, 19, 20, 23, 25),
    "give_z": (25,),
    "a_work": (20, 21, 22, 24, 25, 26, 27, 28),
    "give_core": (28,),
}
ROWS = 2560


def dot(a, b, ca, cb, precision=None):
    return lax.dot_general(
        a, b, (((ca,), (cb,)), ((), ())), preferred_element_type=F32, precision=precision
    )


def iota(shape, dim):
    return lax.broadcasted_iota(jnp.int32, shape, dim)


def place():
    y = lax.axis_index("dp")
    e = lax.axis_index("expert")
    x = lax.div(e, 8)
    z = lax.rem(lax.div(e, 2), 4)
    c = lax.rem(e, 2)
    return y, x, z, c


def dev(y, x, z, c):
    return (lax.rem(y, 4), lax.rem(x, 4) * 8 + lax.rem(z, 4) * 2 + c)


def remote(src, dst, ss, rs, to):
    return pltpu.make_async_remote_copy(
        src_ref=src, dst_ref=dst, send_sem=ss, recv_sem=rs, device_id=to, device_id_type=MESH
    )


def greet(peers):
    bar = pltpu.get_barrier_semaphore()
    for p in peers:
        pl.semaphore_signal(bar, inc=1, device_id=p, device_id_type=MESH)
    pl.semaphore_wait(bar, len(peers))


def dense_gates(ids, logits):
    row = iota((NE, TOK), 0)
    w = jnp.exp(logits[...])
    gates = w / jnp.sum(w, axis=0, keepdims=True)
    chosen = jnp.zeros((NE, TOK), F32)
    dense = jnp.zeros((NE, TOK), F32)
    for k in range(4):
        hit = ids[k : k + 1, :] == row
        chosen = chosen + jnp.where(hit, 1.0, 0.0)
        dense = dense + jnp.where(hit, gates[k : k + 1, :], 0.0)
    upper = jnp.where(iota((TOK, TOK), 0) < iota((TOK, TOK), 1), 1.0, 0.0).astype(BF)
    count = dot(chosen.astype(BF), upper, 1, 0)
    return dense, jnp.where(chosen > 0.0, count, -1.0)


def eye(n):
    return jnp.where(iota((n, n), 0) == iota((n, n), 1), 1.0, 0.0).astype(BF)


def four(ref):
    part = [ref[i].astype(F32) for i in range(4)]
    return ((part[0] + part[1]) + (part[2] + part[3])).astype(BF)


def kernel(
    og_h, ids_h, log_h, ao, pw_h, rw_h, hid_h, w_h,
    dg, total, ra, rc, attn, lg, qt,
    og, ids, logits, pw, rw, hp, yt, za, zc, zs, sb, sa, sc, sss, rsd, rbuf, w, hid, hgt, acc,
    stg, stl, aos, aot, ms, mr, rpo, rpt, s1, cb, zb_, p1, xb_, xg,
    vs, yr, xr, cr, rr, q0, q3,
    a_s, a_r, c_s, c_r, k_s, k_r, g_s, g_r, t_s, t_r, ls,
):
    y, x, z, c = place()
    e = x * 8 + z * 2 + c
    zp = [dev(y, x, z + i, c) for i in (1, 2, 3)]
    xp = [dev(y, x + i, z, c) for i in (1, 2, 3)]
    yp = [dev(y + i, x, z, c) for i in (1, 2, 3)]
    cp = dev(y, x, z, 1 - c)
    yxp = [dev(y + n // 4, x + n % 4, z, c) for n in range(16)]
    zcp = [dev(y, x, z + m // 2, lax.rem(c + m % 2, 2)) for m in range(8)]
    loads = [
        pltpu.make_async_copy(a, b, ls.at[5 + n])
        for n, (a, b) in enumerate(
            [(og_h, og), (ids_h, ids), (log_h, logits), (rw_h, rw), (pw_h, pw), (w_h, w)]
        )
    ]

    def load_hid(b):
        return pltpu.make_async_copy(
            hid_h.at[pl.ds(b * 2, 2)], hp.at[lax.rem(b, 2)], ls.at[11 + lax.rem(b, 2)]
        )

    for l in loads:
        l.start()
    load_hid(0).start()
    load_hid(1).start()
    greet(yxp[1:] + zcp[1:])
    for l in loads[:3]:
        l.wait()
    dense, pos = dense_gates(ids, logits)
    side = [og[MAIN:D, :], pos.astype(BF), dense.astype(BF)]
    yt[0, :, MAIN:DP] = dot(eye(TOK), jnp.concatenate(side, axis=0), 1, 1).astype(BF)

    @pl.loop(NA, NA + NC)
    def _(k):
        rows = pl.ds(pl.multiple_of(k * CH, CH), CH)
        yt[0, :, rows] = dot(eye(TOK), og[rows, :], 1, 1).astype(BF)

    def src_rows(zz, cc):
        return pl.ds(pl.multiple_of((zz * 2 + cc) * TOK, TOK), TOK)

    mine = src_rows(z, c)

    def cols_of(k):
        return pl.ds(pl.multiple_of(k * CH, CH), CH)

    def tok(part, i):
        cols = pl.ds(CB, DP - CB) if part == 0 else pl.ds(0, CB)
        n = part * 4 + i
        return remote(
            yt.at[0, :, cols], yt.at[3 if i == 0 else 1, :, cols], k_s.at[n], k_r.at[n], yp[2 * i]
        )

    def tok_f(part, i):
        cols = pl.ds(CB, DP - CB) if part == 0 else pl.ds(0, CB)
        n = part * 4 + 2 + i
        rows = pl.ds(64 * i, 64)
        return remote(
            yt.at[3 if i == 0 else 1, rows, cols], yt.at[2, rows, cols],
            k_s.at[n], k_r.at[n], yp[2 * i],
        )

    def sections(i):
        to = lax.rem(y + i + 1, 4)
        cols = pl.ds(pl.multiple_of(to * SEC, SEC), SEC)
        return remote(ao.at[:, cols], aos.at[3 - i], k_s.at[8 + i], k_r.at[8 + i], yp[i])

    def own_section():
        cols = pl.ds(pl.multiple_of(y * SEC, SEC), SEC)
        return pltpu.make_async_copy(ao.at[:, cols], aos.at[0], ls.at[13])

    def rp(i):
        return remote(rpo, rpt.at[y], k_s.at[11 + i], k_r.at[11 + i], yp[i])

    def back(i):
        return remote(ms.at[i], mr.at[y], k_s.at[14 + i], k_r.at[14 + i], yp[i])

    def a_z(k, i):
        to = cp if i == 3 else zp[i]
        return remote(
            yt.at[0, :, cols_of(k)], za.at[k, mine], a_s.at[k, i], a_r.at[k, i], to
        )

    def a_own(k):
        return pltpu.make_async_copy(yt.at[0, :, cols_of(k)], za.at[k, mine], a_s.at[k, 14])

    def a_c(k, i):
        part = za.at[k, src_rows(lax.rem(z + 3 - i, 4), c)]
        return remote(part, part, a_s.at[k, 4 + i], a_r.at[k, 4 + i], cp)

    def a_x(k, i):
        to = lax.rem(x + i + 1, 4)
        return remote(
            sa.at[k, to], ra.at[k, y * 4 + x], a_s.at[k, 7 + i], a_r.at[k, 7 + i], xp[i]
        )

    def a_xown(k):
        return pltpu.make_async_copy(sa.at[k, x], ra.at[k, y * 4 + x], a_s.at[k, 15])

    def a_y(k, i):
        part = ra.at[k, pl.ds(y * 4, 4)]
        return remote(part, part, a_s.at[k, 10 + i], a_r.at[k, 10 + i], yp[2 * i])

    def a_f(k, i):
        src = lax.rem(y + (3 if i == 0 else 1), 4)
        part = ra.at[k, pl.ds(src * 4 + 2 * i, 2)]
        return remote(part, part, a_s.at[k, 12 + i], a_r.at[k, 12 + i], yp[2 * i])

    def c_z(j, i):
        to = cp if i == 3 else zp[i]
        return remote(
            yt.at[:, :, cols_of(NA + j)], zc.at[j, :, mine], c_s.at[j, i], c_r.at[j, i], to
        )

    def c_own(j):
        return pltpu.make_async_copy(
            yt.at[:, :, cols_of(NA + j)], zc.at[j, :, mine], c_s.at[j, 14]
        )

    def c_c(j, i):
        part = zc.at[j, :, src_rows(lax.rem(z + 3 - i, 4), c)]
        return remote(part, part, c_s.at[j, 4 + i], c_r.at[j, 4 + i], cp)

    def c_x(j, i):
        to = lax.rem(x + i + 1, 4)
        return remote(
            sc.at[lax.rem(j, 2), to], rc.at[j, :, x], c_s.at[j, 7 + i], c_r.at[j, 7 + i], xp[i]
        )

    def c_xown(j):
        return pltpu.make_async_copy(sc.at[lax.rem(j, 2), x], rc.at[j, :, x], c_s.at[j, 15])

    tail = pl.ds(MAIN, 128)

    def planes(part):
        return pl.ds(0, 1) if part == 0 else pl.ds(1, 3)

    def s_z(part, i):
        to = cp if i == 3 else zp[i]
        n = part * 7 + i
        return remote(
            yt.at[planes(part), :, tail], zs.at[planes(part), mine],
            c_s.at[NC, n], c_r.at[NC, n], to,
        )

    def s_own(part):
        return pltpu.make_async_copy(
            yt.at[planes(part), :, tail], zs.at[planes(part), mine], c_s.at[NC, 14 + part]
        )

    def s_c(part, i):
        n = part * 7 + 4 + i
        piece = zs.at[planes(part), src_rows(lax.rem(z + 3 - i, 4), c)]
        return remote(piece, piece, c_s.at[NC, n], c_r.at[NC, n], cp)

    def s_x(i):
        to = lax.rem(x + i + 1, 4)
        return remote(sss.at[to], rsd.at[:, x], c_s.at[NC + 1, i], c_r.at[NC + 1, i], xp[i])

    def s_xown():
        return pltpu.make_async_copy(sss.at[x], rsd.at[:, x], c_s.at[NC + 1, 14])

    def picks(i):
        row, lane = iota((8, 128), 0), iota((8, 128), 1)
        sel = jnp.where((lane == 64 + row * 8 + z * 2 + c) & (row < 4), 1.0, 0.0).astype(BF)
        slot = dot(sel, zs[i], 1, 1)
        r, t = iota((160, 1024), 0), iota((160, 1024), 1)
        key = jnp.where(
            lax.shift_right_logical(t, 7) == (r & 7), lax.shift_right_logical(r, 3), -5
        ).astype(F32)
        for xx in range(4):
            one = jnp.where(slot[xx : xx + 1, :] == key, 1.0, 0.0).astype(BF)
            sb[i, xx * 160 : (xx + 1) * 160, :] = one

    def g_core():
        there = pl.ds(pl.multiple_of((1 - c) * 256, 256), 256)
        return remote(s1.at[there], cb, g_s.at[0], g_r.at[0], cp)

    def g_z(i):
        to = lax.rem(z + i + 1, 4)
        rows = pl.ds(pl.multiple_of(c * 256 + to * 64, 64), 64)
        return remote(s1.at[rows], zb_.at[i], g_s.at[1 + i], g_r.at[1 + i], zp[i])

    def g_x(i):
        to = lax.rem(x + i + 1, 4)
        rows = pl.ds(pl.multiple_of(to * 16, 16), 16)
        return remote(p1.at[rows], xb_.at[i], g_s.at[4 + i], g_r.at[4 + i], xp[i])

    def h_x(i):
        rows = pl.ds(pl.multiple_of(x * 16, 16), 16)
        return remote(xg.at[rows], xg.at[rows], g_s.at[7 + i], g_r.at[7 + i], xp[i])

    at_z = pl.ds(pl.multiple_of(c * 256 + z * 64, 64), 64)

    def h_z(i):
        return remote(xg, total.at[at_z], g_s.at[10 + i], g_r.at[10 + i], zp[i])

    def h_own():
        return pltpu.make_async_copy(xg, total.at[at_z], g_s.at[14])

    def h_core():
        half = total.at[pl.ds(pl.multiple_of(c * 256, 256), 256)]
        return remote(half, half, g_s.at[13], g_r.at[13], cp)

    def hidden(b):
        return hid[pl.ds(b * 4, 4)].reshape(640, FF)

    def put(slot, k):
        return pltpu.make_async_copy(stg.at[slot], dg.at[:, cols_of(k)], ls.at[slot])

    def put_tail():
        return pltpu.make_async_copy(stl, dg.at[:, pl.ds(MAIN, 64)], ls.at[2])

    def fetch(slot, k, b):
        src = ra.at[k, pl.ds(b * 4, 4)] if slot == 0 else rc.at[k, b]
        return pltpu.make_async_copy(src, rbuf.at[slot, pl.ds(b * 4, 4)], ls.at[16 + slot * 4 + b])

    def work(slot, first, n):
        k = first + n

        @pl.loop(0, 4)
        def _(b):
            rb = pl.ds(pl.multiple_of(b * 640, 640), 640)
            g = dot(hidden(b), w[:, cols_of(k)], 1, 0)
            fetch(slot, n, b).wait()
            prod = g * rbuf[slot, pl.ds(b * 4, 4)].reshape(640, CH).astype(F32)
            acc[rb, :] += prod[:, 0:128] + prod[:, 128:256]

        @pl.when(n > 0)
        def _():
            put(slot, k - 1).wait()

        stg[slot] = dot(hgt[...], rbuf[slot].reshape(ROWS, CH), 1, 0).astype(BF)
        put(slot, k).start()

    for i in range(4):
        s_z(0, i).start()
    s_own(0).start()
    for i in range(2):
        tok(0, i).start()

    @pl.loop(0, NA)
    def _(k):
        rows = pl.ds(pl.multiple_of(k * CH, CH), CH)
        yt[0, :, rows] = dot(eye(TOK), og[rows, :], 1, 1).astype(BF)


    def a_send_z(k):
        for i in range(4):
            a_z(k, i).start()
        a_own(k).start()

    def pick_own(_):
        s_own(0).wait()
        s_z(0, 3).wait_recv()
        for i in range(3):
            s_c(0, i).wait_recv()
        picks(0)

    def attn_part(_):
        @pl.loop(0, 4)
        def _(i):
            got = dot(yt[i, :, 0:D], pw[...], 1, 0).astype(BF)
            ms[lax.rem(i + 3, 4)] = got

        for i in range(3):
            back(i).start()
        mr[y] = ms[3]

    def tok_a_send(_):
        for i in range(2):
            tok(1, i).start()

    def sum_x(_):
        for i in range(3):
            g_x(i).wait_recv()
        rows = pl.ds(pl.multiple_of(x * 16, 16), 16)
        add = p1[rows, :].astype(F32) + xb_[0].astype(F32)
        xg[rows, :] = (add + (xb_[1].astype(F32) + xb_[2].astype(F32))).astype(BF)
        for i in range(3):
            h_x(i).start()

    def c_core(j):
        for i in range(3):
            c_z(j, i).wait_recv()
            c_c(j, i).start()

    def pack_hidden(_):
        @pl.loop(0, CAP // 2)
        def _(b):
            load_hid(b).wait()
            two = [
                dot(eye(TOK), hp[lax.rem(b, 2), h], 1, 1).reshape(16, 8, FF) for h in range(2)
            ]
            rows = pl.ds(pl.multiple_of(b * 16, 16), 16)
            hid[:, rows, :] = jnp.concatenate(two, axis=1).astype(BF)

            @pl.when(b < CAP // 2 - 2)
            def _():
                load_hid(b + 2).start()

        unit = eye(FF)

        @pl.loop(0, 4)
        def _(b):
            rb = pl.ds(pl.multiple_of(b * 640, 640), 640)
            hgt[:, rb] = dot(unit, hidden(b), 1, 1).astype(BF)

        loads[3].wait()
        loads[4].wait()
        loads[5].wait()
        rpo[...] = dot(rw[...], pw[...], 1, 0).astype(BF)
        for i in range(3):
            rp(i).start()
        rpt[y] = rpo[...]

    def tok_c_ring(_):
        for i in range(2):
            tok(0, i).wait_recv()
            tok_f(0, i).start()

    def send_sections(_):
        for i in range(3):
            sections(i).start()
        own_section().start()

    def c_send_z(j):
        for i in range(4):
            c_z(j, i).start()
        c_own(j).start()

    def y_send(k):
        a_xown(k).wait()
        for i in range(3):
            a_x(k, i).wait_recv()
        for i in range(2):
            a_y(k, i).start()

    def sum_z(_):
        for i in range(3):
            g_z(i).wait_recv()
        add = s1[at_z, :].astype(F32) + zb_[0].astype(F32)
        p1[...] = (add + (zb_[1].astype(F32) + zb_[2].astype(F32))).astype(BF)
        for i in range(3):
            g_x(i).start()

    def a_pick(k):
        a_own(k).wait()
        a_z(k, 3).wait_recv()
        for i in range(3):
            a_c(k, i).wait_recv()
        got = dot(sb[0], za[k], 1, 0).astype(BF)
        for xx in range(4):
            sa[k, xx] = got[xx * 160 : (xx + 1) * 160]
        for i in range(3):
            a_x(k, i).start()
        a_xown(k).start()

    def c_work(j):
        c_xown(j).wait()
        for i in range(3):
            c_x(j, i).wait_recv()
        for b in range(4):
            fetch(1, j, b).start()
        work(1, NA, j)

    def tail_pick(_):
        s_own(1).wait()
        s_z(1, 3).wait_recv()
        for i in range(3):
            s_c(1, i).wait_recv()

        @pl.loop(1, 4)
        def _(i):
            picks(i)

        @pl.loop(0, 4)
        def _(i):
            got = dot(sb[i], zs[i], 1, 0).astype(BF)
            for xx in range(4):
                sss[xx, lax.rem(y + i, 4)] = got[xx * 160 : (xx + 1) * 160]

        for i in range(3):
            s_x(i).start()
        s_xown().start()

    def sum_core(_):
        g_core().wait()

        @pl.loop(0, 4)
        def _(b):
            here = pl.ds(pl.multiple_of(c * 256 + b * 64, 64), 64)
            there = pl.ds(pl.multiple_of(b * 64, 64), 64)
            s1[here, :] = (s1[here, :].astype(F32) + cb[there, :].astype(F32)).astype(BF)

        for i in range(3):
            g_z(i).start()

    def tail_core(_):
        for i in range(3):
            s_z(1, i).wait_recv()
            s_c(1, i).start()

    def c_pick(j):
        c_own(j).wait()
        c_z(j, 3).wait_recv()
        for i in range(3):
            c_c(j, i).wait_recv()

        @pl.when(j >= 2)
        def _():
            for i in range(3):
                c_x(j - 2, i).wait_send()

        @pl.loop(0, 4)
        def _(i):
            got = dot(sb[i], zc[j, i], 1, 0).astype(BF)
            for xx in range(4):
                sc[lax.rem(j, 2), xx, lax.rem(y + i, 4)] = got[xx * 160 : (xx + 1) * 160]

        for i in range(3):
            c_x(j, i).start()
        c_xown(j).start()

    def tail_z(_):
        for i in range(2):
            tok_f(0, i).wait_recv()
        for i in range(4):
            s_z(1, i).start()
        s_own(1).start()

    def tok_a_ring(_):
        for i in range(2):
            tok(1, i).wait_recv()
            tok_f(1, i).start()

    def tail_own_core(_):
        for i in range(3):
            s_z(0, i).wait_recv()
            s_c(0, i).start()

    def a_core(k):
        for i in range(3):
            a_z(k, i).wait_recv()
            a_c(k, i).start()

    def gate_hidden(_):
        s_xown().wait()
        for i in range(3):
            s_x(i).wait_recv()
        rows = rsd[...].reshape(ROWS, 128)
        sel = jnp.where(iota((8, 128), 1) == 96 + e, 1.0, 0.0).astype(BF)
        gate = dot(sel, rows, 1, 1)[0:1, :]

        @pl.loop(0, FF // 16)
        def _(b):
            rb = pl.ds(pl.multiple_of(b * 16, 16), 16)
            hgt[rb, :] = (hgt[rb, :].astype(F32) * gate).astype(BF)

        stl[...] = dot(hgt[...], rows, 1, 0)[:, 0:64].astype(BF)
        put_tail().start()
        @pl.loop(0, 4)
        def _(b):
            rb = pl.ds(pl.multiple_of(b * 640, 640), 640)
            g = dot(hidden(b), w[:, MAIN:D], 1, 0)
            part = rsd[b].reshape(640, 128)[:, 0:64].astype(F32)
            acc[rb, :] = jnp.concatenate([g * part, jnp.zeros((640, 64), F32)], axis=1)

    def known_part(_):
        for i in range(2):
            tok_f(1, i).wait_recv()
        own_section().wait()
        for i in range(3):
            sections(i).wait_recv()
        unit = eye(SEC)
        for i in range(4):
            aot[:, i * TOK : (i + 1) * TOK] = dot(unit, aos[i], 1, 1).astype(BF)

        @pl.loop(0, MAIN // CH)
        def _(k):
            block = yt[:, :, cols_of(k)].reshape(4 * TOK, CH)
            s1[:, cols_of(k)] = dot(aot[...], block, 1, 0).astype(BF)

        last = yt[:, :, MAIN:DP].reshape(4 * TOK, 128)
        s1[:, MAIN:D] = dot(aot[...], last, 1, 0)[:, 0:64].astype(BF)
        g_core().start()

    def y_ring(k):
        for i in range(2):
            a_y(k, i).wait_recv()
            a_f(k, i).start()

    def give_z(_):
        for i in range(3):
            h_x(i).wait_recv()
        for i in range(3):
            h_z(i).start()
        h_own().start()

    def a_work(k):
        for i in range(2):
            a_f(k, i).wait_recv()
        for b in range(4):
            fetch(0, k, b).start()
        work(0, 0, k)

    def give_core(_):
        for i in range(3):
            h_z(i).wait_recv()
        h_own().wait()
        h_core().start()

    parts = {
        "a_send_z": a_send_z,
        "pick_own": pick_own,
        "attn_part": attn_part,
        "tok_a_send": tok_a_send,
        "sum_x": sum_x,
        "c_core": c_core,
        "pack_hidden": pack_hidden,
        "tok_c_ring": tok_c_ring,
        "send_sections": send_sections,
        "c_send_z": c_send_z,
        "y_send": y_send,
        "sum_z": sum_z,
        "a_pick": a_pick,
        "c_work": c_work,
        "tail_pick": tail_pick,
        "sum_core": sum_core,
        "tail_core": tail_core,
        "c_pick": c_pick,
        "tail_z": tail_z,
        "tok_a_ring": tok_a_ring,
        "tail_own_core": tail_own_core,
        "a_core": a_core,
        "gate_hidden": gate_hidden,
        "known_part": known_part,
        "y_ring": y_ring,
        "give_z": give_z,
        "a_work": a_work,
        "give_core": give_core,
    }

    @pl.loop(0, STEPS)
    def _(t):
        for key, at in AT.items():
            due = t == at[0]
            number = jnp.int32(0)
            for step in at[1:]:
                due = due | (t == step)
                number = number + jnp.where(t >= step, 1, 0)

            @pl.when(due)
            def _(part=parts[key], number=number):
                part(number)

    at_slot = iota((4, CAP, 8, 128), 3) == iota((4, CAP, 8, 128), 1)
    for b in range(4):
        block = acc[b * 640 : (b + 1) * 640, :].reshape(4, CAP, 8, 128)
        sums = jnp.sum(block, axis=3, keepdims=True)
        vs[b] = jnp.sum(jnp.where(at_slot, sums, 0.0), axis=1)

    def v_yx(n):
        block = vs.at[lax.rem(y + n // 4, 4), lax.rem(x + n % 4, 4)]
        return remote(block, yr.at[n], t_s.at[n], t_r.at[n], yxp[n])

    def v_zc(m):
        return remote(xr, cr.at[:, z, c], t_s.at[16 + m], t_r.at[16 + m], zcp[m])

    def r_y(i):
        return remote(rr.at[0], rr.at[3 - i], t_s.at[24 + i], t_r.at[24 + i], yp[i])

    def q_zc(m):
        return remote(q0.at[0], q0.at[m], t_s.at[27 + m], t_r.at[27 + m], zcp[m])

    def q_x(i):
        return remote(q3.at[0], q3.at[1 + i], t_s.at[35 + i], t_r.at[35 + i], xp[i])

    for n in range(1, 16):
        v_yx(n).start()
    yr[0] = vs[y, x]
    for n in range(1, 16):
        v_yx(n).wait()
    for n in range(4):
        xr[lax.rem(x + 4 - n, 4)] = (yr[n] + yr[4 + n]) + (yr[8 + n] + yr[12 + n])
    for m in range(1, 8):
        v_zc(m).start()
    cr[:, z, c] = xr[...]
    for m in range(1, 8):
        v_zc(m).wait()
    got = cr[...].reshape(NE, 8, 128)
    got = jnp.sum(jnp.where(iota((NE, 8, 128), 1) == z * 2 + c, got, 0.0), axis=1)
    grad = jnp.zeros((NE, TOK), F32)
    for s in range(CAP):
        grad = grad + jnp.where(pos == s, got[:, s : s + 1], 0.0)
    inner = jnp.sum(dense * grad, axis=0, keepdims=True)
    full = dense * (grad - inner)
    rrow = full.astype(BF)
    rr[0] = rrow
    for i in range(3):
        r_y(i).start()
    row = iota((NE, TOK), 0)
    for k in range(4):
        hit = ids[k : k + 1, :] == row
        lg[k : k + 1, :] = jnp.sum(jnp.where(hit, full, 0.0), axis=0, keepdims=True)
    for i in range(3):
        r_y(i).wait()
    q = jnp.zeros((NE, SEC), F32)
    for t in range(4):
        q = q + dot(rr[t], aos[t], 1, 0)
    q0[0] = q.astype(BF)
    for m in range(1, 8):
        q_zc(m).start()
    for i in range(3):
        rp(i).wait()
        back(i).wait()
    for t in range(4):
        more = dot(rrow, rpt[t], 0, 0)
        attn[:, t * SEC : (t + 1) * SEC] = (mr[t].astype(F32) + more).astype(BF)
    for m in range(1, 8):
        q_zc(m).wait()
    eight = [q0[m].astype(F32) for m in range(8)]
    while len(eight) > 1:
        eight = [eight[m] + eight[m + 1] for m in range(0, len(eight), 2)]
    q3[0] = eight[0].astype(BF)
    for i in range(3):
        q_x(i).start()
    for i in range(3):
        q_x(i).wait()
    qt[...] = four(q3)

    put(0, NA - 1).wait()
    put(1, NA + NC - 1).wait()
    put_tail().wait()
    h_core().wait()
    for i in range(2):
        for part in range(2):
            tok(part, i).wait_send()
            tok_f(part, i).wait_send()
    for i in range(3):
        sections(i).wait_send()
        g_z(i).wait_send()
        g_x(i).wait_send()
        h_x(i).wait_send()
        h_z(i).wait_send()
        s_x(i).wait_send()
    for part in range(2):
        for i in range(4):
            s_z(part, i).wait_send()
        for i in range(3):
            s_c(part, i).wait_send()

    @pl.loop(0, NA)
    def _(k):
        for i in range(4):
            a_z(k, i).wait_send()
        for i in range(3):
            a_c(k, i).wait_send()
            a_x(k, i).wait_send()
        for i in range(2):
            a_y(k, i).wait_send()
            a_f(k, i).wait_send()

    @pl.loop(0, NC)
    def _(j):
        for i in range(4):
            c_z(j, i).wait_send()
        for i in range(3):
            c_c(j, i).wait_send()

        @pl.when(j >= NC - 2)
        def _():
            for i in range(3):
                c_x(j, i).wait_send()


def local(
    out_grad, expert_ids, chosen_logits, router_weight, hidden_act, down_weight, attn_out, proj_weight
):
    vm = pl.BlockSpec(memory_space=pltpu.VMEM)
    hbm = pl.BlockSpec(memory_space=pl.ANY)
    sds = jax.ShapeDtypeStruct
    sem = pltpu.SemaphoreType.DMA
    v = pltpu.VMEM
    dg, total, _, _, attn, lg, qt = pl.pallas_call(
        kernel,
        out_shape=(
            sds((FF, D), BF), sds((SEC, D), BF), sds((NA, 16, 160, CH), BF),
            sds((NC, 4, 4, 160, CH), BF), sds((TOK, HID), BF), sds((4, TOK), F32),
            sds((NE, SEC), BF),
        ),
        in_specs=[hbm] * 8,
        out_specs=(hbm, hbm, hbm, hbm, vm, vm, vm),
        scratch_shapes=[
            v((D, TOK), BF), v((4, TOK), jnp.int32), v((4, TOK), F32), v((D, SEC), BF),
            v((NE, D), BF), v((2, 2, FF, TOK), BF), v((4, TOK, DP), BF),
            v((NA, 1024, CH), BF), v((NC, 4, 1024, CH), BF), v((4, 1024, 128), BF),
            v((4, 640, 1024), BF), v((NA, 4, 160, CH), BF), v((2, 4, 4, 160, CH), BF),
            v((4, 4, 160, 128), BF), v((4, 4, 160, 128), BF), v((2, 16, 160, CH), BF),
            v((FF, D), BF), v((16, 160, FF), BF), v((FF, ROWS), BF),
            v((ROWS, 128), F32), v((2, FF, CH), BF), v((FF, 64), BF),
            v((4, TOK, SEC), BF), v((SEC, SEC), BF), v((4, TOK, SEC), BF), v((4, TOK, SEC), BF),
            v((NE, SEC), BF), v((4, NE, SEC), BF), v((SEC, D), BF), v((256, D), BF),
            v((3, 64, D), BF), v((64, D), BF), v((3, 16, D), BF), v((64, D), BF),
            v((4, 4, 8, 128), F32), v((16, 8, 128), F32), v((4, 8, 128), F32),
            v((4, 4, 2, 8, 128), F32), v((4, NE, TOK), BF),
            v((8, NE, SEC), BF), v((4, NE, SEC), BF),
            sem((NA, 16)), sem((NA, 16)), sem((NC + 2, 16)), sem((NC + 2, 16)),
            sem((17,)), sem((17,)), sem((15,)), sem((15,)), sem((40,)), sem((40,)), sem((32,)),
        ],
        compiler_params=pltpu.CompilerParams(
            collective_id=0, has_side_effects=True, vmem_limit_bytes=62 * 2**20
        ),
        cost_estimate=pl.CostEstimate(
            flops=50 * 10**9, bytes_accessed=400 * 10**6, transcendentals=0
        ),
        name="layer_backward",
    )(
        out_grad.T, expert_ids.T, chosen_logits.T, attn_out, proj_weight.T, router_weight.T,
        jnp.transpose(hidden_act[0], (1, 2, 0)), down_weight[0],
    )
    more = dot(qt, router_weight, 0, 1)
    proj_grad = (total.astype(F32) + more).astype(BF)
    return attn, proj_grad, dg[None], lg.T


def solution(mesh):
    return jax.shard_map(
        local,
        mesh=mesh,
        in_specs=(
            P(("dp", "expert"), None),
            P(("dp", "expert"), None),
            P(("dp", "expert"), None),
            P(),
            P("expert", None, None, "dp"),
            P("expert", "dp", None),
            P(("dp", "expert"), None),
            P("dp", None),
        ),
        out_specs=(
            P(("dp", "expert"), None),
            P("dp", None),
            P("expert", "dp", None),
            P(("dp", "expert"), None),
        ),
        check_vma=False,
    )
```

```python
import functools

import jax
import jax.numpy as jnp
from jax import lax
from jax.experimental import pallas as pl
from jax.experimental.pallas import tpu as pltpu
from jax.sharding import PartitionSpec as P

MESH = pl.DeviceIdType.MESH
BF = jnp.bfloat16
F32 = jnp.float32
D = 2880
DP = 2944
MAIN = 2816
FF = 720
TOK = 128
NE = 32
CAP = 20
SEC = 512
HID = 2048
CH = 256
NA = 8
NC = 3
CB = NA * CH
STEPS = 29
AT = {
    "a_send_z": (0, 1, 2, 3, 5, 6, 8, 9),
    "pick_own": (3,),
    "attn_part": (17,),
    "tok_a_send": (1,),
    "sum_x": (24,),
    "c_core": (15, 19, 23),
    "pack_hidden": (1,),
    "tok_c_ring": (1,),
    "send_sections": (5,),
    "c_send_z": (7, 15, 19),
    "y_send": (6, 7, 10, 12, 13, 14, 19, 20),
    "sum_z": (21,),
    "a_pick": (3, 4, 6, 9, 10, 11, 17, 18),
    "c_work": (21, 23, 28),
    "tail_pick": (14,),
    "sum_core": (15,),
    "tail_core": (11,),
    "c_pick": (18, 20, 24),
    "tail_z": (6,),
    "tok_a_ring": (5,),
    "tail_own_core": (1,),
    "a_core": (1, 2, 4, 5, 7, 8, 15, 16),
    "gate_hidden": (19,),
    "known_part": (11,),
    "y_ring": (11, 14, 16, 18, 19, 20, 23, 25),
    "give_z": (25,),
    "a_work": (20, 21, 22, 24, 25, 26, 27, 28),
    "give_core": (28,),
}
ROWS = 2560


def dot(a, b, ca, cb, precision=None):
    return lax.dot_general(
        a, b, (((ca,), (cb,)), ((), ())), preferred_element_type=F32, precision=precision
    )


def iota(shape, dim):
    return lax.broadcasted_iota(jnp.int32, shape, dim)


def place():
    y = lax.axis_index("dp")
    e = lax.axis_index("expert")
    x = lax.div(e, 8)
    z = lax.rem(lax.div(e, 2), 4)
    c = lax.rem(e, 2)
    return y, x, z, c


def dev(y, x, z, c):
    return (lax.rem(y, 4), lax.rem(x, 4) * 8 + lax.rem(z, 4) * 2 + c)


def remote(src, dst, ss, rs, to):
    return pltpu.make_async_remote_copy(
        src_ref=src, dst_ref=dst, send_sem=ss, recv_sem=rs, device_id=to, device_id_type=MESH
    )


def greet(peers):
    bar = pltpu.get_barrier_semaphore()
    for p in peers:
        pl.semaphore_signal(bar, inc=1, device_id=p, device_id_type=MESH)
    pl.semaphore_wait(bar, len(peers))


def dense_gates(ids, logits):
    row = iota((NE, TOK), 0)
    w = jnp.exp(logits[...])
    gates = w / jnp.sum(w, axis=0, keepdims=True)
    chosen = jnp.zeros((NE, TOK), F32)
    dense = jnp.zeros((NE, TOK), F32)
    for k in range(4):
        hit = ids[k : k + 1, :] == row
        chosen = chosen + jnp.where(hit, 1.0, 0.0)
        dense = dense + jnp.where(hit, gates[k : k + 1, :], 0.0)
    upper = jnp.where(iota((TOK, TOK), 0) < iota((TOK, TOK), 1), 1.0, 0.0).astype(BF)
    count = dot(chosen.astype(BF), upper, 1, 0)
    return dense, jnp.where(chosen > 0.0, count, -1.0)


def eye(n):
    return jnp.where(iota((n, n), 0) == iota((n, n), 1), 1.0, 0.0).astype(BF)


def four(ref):
    part = [ref[i].astype(F32) for i in range(4)]
    return ((part[0] + part[1]) + (part[2] + part[3])).astype(BF)


def kernel(
    og_h, ids_h, log_h, ao, pw_h, rw_h, hid_h, w_h,
    dg, total, ra, rc, attn, lg, qt,
    og, ids, logits, pw, rw, hp, yt, za, zc, zs, sb, sa, sc, sss, rsd, rbuf, w, hid, hgt, acc,
    stg, stl, aos, aot, ms, mr, rpo, rpt, s1, cb, zb_, p1, xb_, xg,
    vs, yr, xr, cr, rr, q0, q3,
    a_s, a_r, c_s, c_r, k_s, k_r, g_s, g_r, t_s, t_r, ls,
):
    y, x, z, c = place()
    e = x * 8 + z * 2 + c
    zp = [dev(y, x, z + i, c) for i in (1, 2, 3)]
    xp = [dev(y, x + i, z, c) for i in (1, 2, 3)]
    yp = [dev(y + i, x, z, c) for i in (1, 2, 3)]
    cp = dev(y, x, z, 1 - c)
    yxp = [dev(y + n // 4, x + n % 4, z, c) for n in range(16)]
    zcp = [dev(y, x, z + m // 2, lax.rem(c + m % 2, 2)) for m in range(8)]
    loads = [
        pltpu.make_async_copy(a, b, ls.at[5 + n])
        for n, (a, b) in enumerate(
            [(og_h, og), (ids_h, ids), (log_h, logits), (rw_h, rw), (pw_h, pw), (w_h, w)]
        )
    ]

    def load_hid(b):
        return pltpu.make_async_copy(
            hid_h.at[pl.ds(b * 2, 2)], hp.at[lax.rem(b, 2)], ls.at[11 + lax.rem(b, 2)]
        )

    for l in loads:
        l.start()
    load_hid(0).start()
    load_hid(1).start()
    greet(yxp[1:] + zcp[1:])
    for l in loads[:3]:
        l.wait()
    dense, pos = dense_gates(ids, logits)
    side = [og[MAIN:D, :], pos.astype(BF), dense.astype(BF)]
    yt[0, :, MAIN:DP] = dot(eye(TOK), jnp.concatenate(side, axis=0), 1, 1).astype(BF)

    @pl.loop(NA, NA + NC)
    def _(k):
        rows = pl.ds(pl.multiple_of(k * CH, CH), CH)
        yt[0, :, rows] = dot(eye(TOK), og[rows, :], 1, 1).astype(BF)

    def src_rows(zz, cc):
        return pl.ds(pl.multiple_of((zz * 2 + cc) * TOK, TOK), TOK)

    mine = src_rows(z, c)

    def cols_of(k):
        return pl.ds(pl.multiple_of(k * CH, CH), CH)

    def tok(part, i):
        cols = pl.ds(CB, DP - CB) if part == 0 else pl.ds(0, CB)
        n = part * 4 + i
        return remote(
            yt.at[0, :, cols], yt.at[3 if i == 0 else 1, :, cols], k_s.at[n], k_r.at[n], yp[2 * i]
        )

    def tok_f(part, i):
        cols = pl.ds(CB, DP - CB) if part == 0 else pl.ds(0, CB)
        n = part * 4 + 2 + i
        rows = pl.ds(64 * i, 64)
        return remote(
            yt.at[3 if i == 0 else 1, rows, cols], yt.at[2, rows, cols],
            k_s.at[n], k_r.at[n], yp[2 * i],
        )

    def sections(i):
        to = lax.rem(y + i + 1, 4)
        cols = pl.ds(pl.multiple_of(to * SEC, SEC), SEC)
        return remote(ao.at[:, cols], aos.at[3 - i], k_s.at[8 + i], k_r.at[8 + i], yp[i])

    def own_section():
        cols = pl.ds(pl.multiple_of(y * SEC, SEC), SEC)
        return pltpu.make_async_copy(ao.at[:, cols], aos.at[0], ls.at[13])

    def rp(i):
        return remote(rpo, rpt.at[y], k_s.at[11 + i], k_r.at[11 + i], yp[i])

    def back(i):
        return remote(ms.at[i], mr.at[y], k_s.at[14 + i], k_r.at[14 + i], yp[i])

    def a_z(k, i):
        to = cp if i == 3 else zp[i]
        return remote(
            yt.at[0, :, cols_of(k)], za.at[k, mine], a_s.at[k, i], a_r.at[k, i], to
        )

    def a_own(k):
        return pltpu.make_async_copy(yt.at[0, :, cols_of(k)], za.at[k, mine], a_s.at[k, 14])

    def a_c(k, i):
        part = za.at[k, src_rows(lax.rem(z + 3 - i, 4), c)]
        return remote(part, part, a_s.at[k, 4 + i], a_r.at[k, 4 + i], cp)

    def a_x(k, i):
        to = lax.rem(x + i + 1, 4)
        return remote(
            sa.at[k, to], ra.at[k, y * 4 + x], a_s.at[k, 7 + i], a_r.at[k, 7 + i], xp[i]
        )

    def a_xown(k):
        return pltpu.make_async_copy(sa.at[k, x], ra.at[k, y * 4 + x], a_s.at[k, 15])

    def a_y(k, i):
        part = ra.at[k, pl.ds(y * 4, 4)]
        return remote(part, part, a_s.at[k, 10 + i], a_r.at[k, 10 + i], yp[2 * i])

    def a_f(k, i):
        src = lax.rem(y + (3 if i == 0 else 1), 4)
        part = ra.at[k, pl.ds(src * 4 + 2 * i, 2)]
        return remote(part, part, a_s.at[k, 12 + i], a_r.at[k, 12 + i], yp[2 * i])

    def c_z(j, i):
        to = cp if i == 3 else zp[i]
        return remote(
            yt.at[:, :, cols_of(NA + j)], zc.at[j, :, mine], c_s.at[j, i], c_r.at[j, i], to
        )

    def c_own(j):
        return pltpu.make_async_copy(
            yt.at[:, :, cols_of(NA + j)], zc.at[j, :, mine], c_s.at[j, 14]
        )

    def c_c(j, i):
        part = zc.at[j, :, src_rows(lax.rem(z + 3 - i, 4), c)]
        return remote(part, part, c_s.at[j, 4 + i], c_r.at[j, 4 + i], cp)

    def c_x(j, i):
        to = lax.rem(x + i + 1, 4)
        return remote(
            sc.at[lax.rem(j, 2), to], rc.at[j, :, x], c_s.at[j, 7 + i], c_r.at[j, 7 + i], xp[i]
        )

    def c_xown(j):
        return pltpu.make_async_copy(sc.at[lax.rem(j, 2), x], rc.at[j, :, x], c_s.at[j, 15])

    tail = pl.ds(MAIN, 128)

    def planes(part):
        return pl.ds(0, 1) if part == 0 else pl.ds(1, 3)

    def s_z(part, i):
        to = cp if i == 3 else zp[i]
        n = part * 7 + i
        return remote(
            yt.at[planes(part), :, tail], zs.at[planes(part), mine],
            c_s.at[NC, n], c_r.at[NC, n], to,
        )

    def s_own(part):
        return pltpu.make_async_copy(
            yt.at[planes(part), :, tail], zs.at[planes(part), mine], c_s.at[NC, 14 + part]
        )

    def s_c(part, i):
        n = part * 7 + 4 + i
        piece = zs.at[planes(part), src_rows(lax.rem(z + 3 - i, 4), c)]
        return remote(piece, piece, c_s.at[NC, n], c_r.at[NC, n], cp)

    def s_x(i):
        to = lax.rem(x + i + 1, 4)
        return remote(sss.at[to], rsd.at[:, x], c_s.at[NC + 1, i], c_r.at[NC + 1, i], xp[i])

    def s_xown():
        return pltpu.make_async_copy(sss.at[x], rsd.at[:, x], c_s.at[NC + 1, 14])

    def picks(i):
        row, lane = iota((8, 128), 0), iota((8, 128), 1)
        sel = jnp.where((lane == 64 + row * 8 + z * 2 + c) & (row < 4), 1.0, 0.0).astype(BF)
        slot = dot(sel, zs[i], 1, 1)
        r, t = iota((160, 1024), 0), iota((160, 1024), 1)
        key = jnp.where(
            lax.shift_right_logical(t, 7) == (r & 7), lax.shift_right_logical(r, 3), -5
        ).astype(F32)
        for xx in range(4):
            one = jnp.where(slot[xx : xx + 1, :] == key, 1.0, 0.0).astype(BF)
            sb[i, xx * 160 : (xx + 1) * 160, :] = one

    def g_core():
        there = pl.ds(pl.multiple_of((1 - c) * 256, 256), 256)
        return remote(s1.at[there], cb, g_s.at[0], g_r.at[0], cp)

    def g_z(i):
        to = lax.rem(z + i + 1, 4)
        rows = pl.ds(pl.multiple_of(c * 256 + to * 64, 64), 64)
        return remote(s1.at[rows], zb_.at[i], g_s.at[1 + i], g_r.at[1 + i], zp[i])

    def g_x(i):
        to = lax.rem(x + i + 1, 4)
        rows = pl.ds(pl.multiple_of(to * 16, 16), 16)
        return remote(p1.at[rows], xb_.at[i], g_s.at[4 + i], g_r.at[4 + i], xp[i])

    def h_x(i):
        rows = pl.ds(pl.multiple_of(x * 16, 16), 16)
        return remote(xg.at[rows], xg.at[rows], g_s.at[7 + i], g_r.at[7 + i], xp[i])

    at_z = pl.ds(pl.multiple_of(c * 256 + z * 64, 64), 64)

    def h_z(i):
        return remote(xg, total.at[at_z], g_s.at[10 + i], g_r.at[10 + i], zp[i])

    def h_own():
        return pltpu.make_async_copy(xg, total.at[at_z], g_s.at[14])

    def h_core():
        half = total.at[pl.ds(pl.multiple_of(c * 256, 256), 256)]
        return remote(half, half, g_s.at[13], g_r.at[13], cp)

    def hidden(b):
        return hid[pl.ds(b * 4, 4)].reshape(640, FF)

    def put(slot, k):
        return pltpu.make_async_copy(stg.at[slot], dg.at[:, cols_of(k)], ls.at[slot])

    def put_tail():
        return pltpu.make_async_copy(stl, dg.at[:, pl.ds(MAIN, 64)], ls.at[2])

    def fetch(slot, k, b):
        src = ra.at[k, pl.ds(b * 4, 4)] if slot == 0 else rc.at[k, b]
        return pltpu.make_async_copy(src, rbuf.at[slot, pl.ds(b * 4, 4)], ls.at[16 + slot * 4 + b])

    def work(slot, first, n):
        k = first + n

        @pl.loop(0, 4)
        def _(turn):
            b = lax.rem(y + 3 + turn, 4)
            rb = pl.ds(pl.multiple_of(b * 640, 640), 640)
            g = dot(hidden(b), w[:, cols_of(k)], 1, 0)
            fetch(slot, n, b).wait()
            prod = g * rbuf[slot, pl.ds(b * 4, 4)].reshape(640, CH).astype(F32)
            acc[rb, :] += prod[:, 0:128] + prod[:, 128:256]

        @pl.when(n > 0)
        def _():
            put(slot, k - 1).wait()

        stg[slot] = dot(hgt[...], rbuf[slot].reshape(ROWS, CH), 1, 0).astype(BF)
        put(slot, k).start()

    for i in range(4):
        s_z(0, i).start()
    s_own(0).start()
    for i in range(2):
        tok(0, i).start()

    @pl.loop(0, NA)
    def _(k):
        rows = pl.ds(pl.multiple_of(k * CH, CH), CH)
        yt[0, :, rows] = dot(eye(TOK), og[rows, :], 1, 1).astype(BF)


    def a_send_z(k):
        for i in range(4):
            a_z(k, i).start()
        a_own(k).start()

    def pick_own(_):
        s_own(0).wait()
        s_z(0, 3).wait_recv()
        for i in range(3):
            s_c(0, i).wait_recv()
        picks(0)

    def attn_part(_):
        @pl.loop(0, 4)
        def _(i):
            got = dot(yt[i, :, 0:D], pw[...], 1, 0).astype(BF)
            ms[lax.rem(i + 3, 4)] = got

        for i in range(3):
            back(i).start()
        mr[y] = ms[3]

    def tok_a_send(_):
        for i in range(2):
            tok(1, i).start()

    def sum_x(_):
        for i in range(3):
            g_x(i).wait_recv()
        rows = pl.ds(pl.multiple_of(x * 16, 16), 16)
        add = p1[rows, :].astype(F32) + xb_[0].astype(F32)
        xg[rows, :] = (add + (xb_[1].astype(F32) + xb_[2].astype(F32))).astype(BF)
        for i in range(3):
            h_x(i).start()

    def c_core(j):
        for i in range(3):
            c_z(j, i).wait_recv()
            c_c(j, i).start()

    def pack_hidden(_):
        @pl.loop(0, CAP // 2)
        def _(b):
            load_hid(b).wait()
            two = [
                dot(eye(TOK), hp[lax.rem(b, 2), h], 1, 1).reshape(16, 8, FF) for h in range(2)
            ]
            rows = pl.ds(pl.multiple_of(b * 16, 16), 16)
            hid[:, rows, :] = jnp.concatenate(two, axis=1).astype(BF)

            @pl.when(b < CAP // 2 - 2)
            def _():
                load_hid(b + 2).start()

        unit = eye(FF)

        @pl.loop(0, 4)
        def _(b):
            rb = pl.ds(pl.multiple_of(b * 640, 640), 640)
            hgt[:, rb] = dot(unit, hidden(b), 1, 1).astype(BF)

        loads[3].wait()
        loads[4].wait()
        loads[5].wait()
        rpo[...] = dot(rw[...], pw[...], 1, 0).astype(BF)
        for i in range(3):
            rp(i).start()
        rpt[y] = rpo[...]

    def tok_c_ring(_):
        for i in range(2):
            tok(0, i).wait_recv()
            tok_f(0, i).start()

    def send_sections(_):
        for i in range(3):
            sections(i).start()
        own_section().start()

    def c_send_z(j):
        for i in range(4):
            c_z(j, i).start()
        c_own(j).start()

    def y_send(k):
        a_xown(k).wait()
        for i in range(3):
            a_x(k, i).wait_recv()
        for i in range(2):
            a_y(k, i).start()

    def sum_z(_):
        for i in range(3):
            g_z(i).wait_recv()
        add = s1[at_z, :].astype(F32) + zb_[0].astype(F32)
        p1[...] = (add + (zb_[1].astype(F32) + zb_[2].astype(F32))).astype(BF)
        for i in range(3):
            g_x(i).start()

    def a_pick(k):
        a_own(k).wait()
        a_z(k, 3).wait_recv()
        for i in range(3):
            a_c(k, i).wait_recv()
        got = dot(sb[0], za[k], 1, 0).astype(BF)
        for xx in range(4):
            sa[k, xx] = got[xx * 160 : (xx + 1) * 160]
        for i in range(3):
            a_x(k, i).start()
        a_xown(k).start()

    def c_work(j):
        c_xown(j).wait()
        for i in range(3):
            c_x(j, i).wait_recv()
        for b in range(4):
            fetch(1, j, b).start()
        work(1, NA, j)

    def tail_pick(_):
        s_own(1).wait()
        s_z(1, 3).wait_recv()
        for i in range(3):
            s_c(1, i).wait_recv()

        @pl.loop(1, 4)
        def _(i):
            picks(i)

        @pl.loop(0, 4)
        def _(i):
            got = dot(sb[i], zs[i], 1, 0).astype(BF)
            for xx in range(4):
                sss[xx, lax.rem(y + i, 4)] = got[xx * 160 : (xx + 1) * 160]

        for i in range(3):
            s_x(i).start()
        s_xown().start()

    def sum_core(_):
        g_core().wait()

        @pl.loop(0, 4)
        def _(b):
            here = pl.ds(pl.multiple_of(c * 256 + b * 64, 64), 64)
            there = pl.ds(pl.multiple_of(b * 64, 64), 64)
            s1[here, :] = (s1[here, :].astype(F32) + cb[there, :].astype(F32)).astype(BF)

        for i in range(3):
            g_z(i).start()

    def tail_core(_):
        for i in range(3):
            s_z(1, i).wait_recv()
            s_c(1, i).start()

    def c_pick(j):
        c_own(j).wait()
        c_z(j, 3).wait_recv()
        for i in range(3):
            c_c(j, i).wait_recv()

        @pl.when(j >= 2)
        def _():
            for i in range(3):
                c_x(j - 2, i).wait_send()

        @pl.loop(0, 4)
        def _(i):
            got = dot(sb[i], zc[j, i], 1, 0).astype(BF)
            for xx in range(4):
                sc[lax.rem(j, 2), xx, lax.rem(y + i, 4)] = got[xx * 160 : (xx + 1) * 160]

        for i in range(3):
            c_x(j, i).start()
        c_xown(j).start()

    def tail_z(_):
        for i in range(2):
            tok_f(0, i).wait_recv()
        for i in range(4):
            s_z(1, i).start()
        s_own(1).start()

    def tok_a_ring(_):
        for i in range(2):
            tok(1, i).wait_recv()
            tok_f(1, i).start()

    def tail_own_core(_):
        for i in range(3):
            s_z(0, i).wait_recv()
            s_c(0, i).start()

    def a_core(k):
        for i in range(3):
            a_z(k, i).wait_recv()
            a_c(k, i).start()

    def gate_hidden(_):
        s_xown().wait()
        for i in range(3):
            s_x(i).wait_recv()
        rows = rsd[...].reshape(ROWS, 128)
        sel = jnp.where(iota((8, 128), 1) == 96 + e, 1.0, 0.0).astype(BF)
        gate = dot(sel, rows, 1, 1)[0:1, :]

        @pl.loop(0, FF // 16)
        def _(b):
            rb = pl.ds(pl.multiple_of(b * 16, 16), 16)
            hgt[rb, :] = (hgt[rb, :].astype(F32) * gate).astype(BF)

        stl[...] = dot(hgt[...], rows, 1, 0)[:, 0:64].astype(BF)
        put_tail().start()
        @pl.loop(0, 4)
        def _(b):
            rb = pl.ds(pl.multiple_of(b * 640, 640), 640)
            g = dot(hidden(b), w[:, MAIN:D], 1, 0)
            part = rsd[b].reshape(640, 128)[:, 0:64].astype(F32)
            acc[rb, :] = jnp.concatenate([g * part, jnp.zeros((640, 64), F32)], axis=1)

    def known_part(_):
        for i in range(2):
            tok_f(1, i).wait_recv()
        own_section().wait()
        for i in range(3):
            sections(i).wait_recv()
        unit = eye(SEC)
        for i in range(4):
            aot[:, i * TOK : (i + 1) * TOK] = dot(unit, aos[i], 1, 1).astype(BF)

        @pl.loop(0, MAIN // CH)
        def _(k):
            block = yt[:, :, cols_of(k)].reshape(4 * TOK, CH)
            s1[:, cols_of(k)] = dot(aot[...], block, 1, 0).astype(BF)

        last = yt[:, :, MAIN:DP].reshape(4 * TOK, 128)
        s1[:, MAIN:D] = dot(aot[...], last, 1, 0)[:, 0:64].astype(BF)
        g_core().start()

    def y_ring(k):
        for i in range(2):
            a_y(k, i).wait_recv()
            a_f(k, i).start()

    def give_z(_):
        for i in range(3):
            h_x(i).wait_recv()
        for i in range(3):
            h_z(i).start()
        h_own().start()

    def a_work(k):
        for n in (3, 0, 1):
            fetch(0, k, lax.rem(y + n, 4)).start()
        for i in range(2):
            a_f(k, i).wait_recv()
        fetch(0, k, lax.rem(y + 2, 4)).start()
        work(0, 0, k)

    def give_core(_):
        for i in range(3):
            h_z(i).wait_recv()
        h_own().wait()
        h_core().start()

    parts = {
        "a_send_z": a_send_z,
        "pick_own": pick_own,
        "attn_part": attn_part,
        "tok_a_send": tok_a_send,
        "sum_x": sum_x,
        "c_core": c_core,
        "pack_hidden": pack_hidden,
        "tok_c_ring": tok_c_ring,
        "send_sections": send_sections,
        "c_send_z": c_send_z,
        "y_send": y_send,
        "sum_z": sum_z,
        "a_pick": a_pick,
        "c_work": c_work,
        "tail_pick": tail_pick,
        "sum_core": sum_core,
        "tail_core": tail_core,
        "c_pick": c_pick,
        "tail_z": tail_z,
        "tok_a_ring": tok_a_ring,
        "tail_own_core": tail_own_core,
        "a_core": a_core,
        "gate_hidden": gate_hidden,
        "known_part": known_part,
        "y_ring": y_ring,
        "give_z": give_z,
        "a_work": a_work,
        "give_core": give_core,
    }

    @pl.loop(0, STEPS)
    def _(t):
        for key, at in AT.items():
            due = t == at[0]
            number = jnp.int32(0)
            for step in at[1:]:
                due = due | (t == step)
                number = number + jnp.where(t >= step, 1, 0)

            @pl.when(due)
            def _(part=parts[key], number=number):
                part(number)

    at_slot = iota((4, CAP, 8, 128), 3) == iota((4, CAP, 8, 128), 1)
    for b in range(4):
        block = acc[b * 640 : (b + 1) * 640, :].reshape(4, CAP, 8, 128)
        sums = jnp.sum(block, axis=3, keepdims=True)
        vs[b] = jnp.sum(jnp.where(at_slot, sums, 0.0), axis=1)

    def v_yx(n):
        block = vs.at[lax.rem(y + n // 4, 4), lax.rem(x + n % 4, 4)]
        return remote(block, yr.at[n], t_s.at[n], t_r.at[n], yxp[n])

    def v_zc(m):
        return remote(xr, cr.at[:, z, c], t_s.at[16 + m], t_r.at[16 + m], zcp[m])

    def r_y(i):
        return remote(rr.at[0], rr.at[3 - i], t_s.at[24 + i], t_r.at[24 + i], yp[i])

    def q_zc(m):
        return remote(q0.at[0], q0.at[m], t_s.at[27 + m], t_r.at[27 + m], zcp[m])

    def q_x(i):
        return remote(q3.at[0], q3.at[1 + i], t_s.at[35 + i], t_r.at[35 + i], xp[i])

    for n in range(1, 16):
        v_yx(n).start()
    yr[0] = vs[y, x]
    for n in range(1, 16):
        v_yx(n).wait()
    for n in range(4):
        xr[lax.rem(x + 4 - n, 4)] = (yr[n] + yr[4 + n]) + (yr[8 + n] + yr[12 + n])
    for m in range(1, 8):
        v_zc(m).start()
    cr[:, z, c] = xr[...]
    for m in range(1, 8):
        v_zc(m).wait()
    got = cr[...].reshape(NE, 8, 128)
    got = jnp.sum(jnp.where(iota((NE, 8, 128), 1) == z * 2 + c, got, 0.0), axis=1)
    grad = jnp.zeros((NE, TOK), F32)
    for s in range(CAP):
        grad = grad + jnp.where(pos == s, got[:, s : s + 1], 0.0)
    inner = jnp.sum(dense * grad, axis=0, keepdims=True)
    full = dense * (grad - inner)
    rrow = full.astype(BF)
    rr[0] = rrow
    for i in range(3):
        r_y(i).start()
    row = iota((NE, TOK), 0)
    for k in range(4):
        hit = ids[k : k + 1, :] == row
        lg[k : k + 1, :] = jnp.sum(jnp.where(hit, full, 0.0), axis=0, keepdims=True)
    for i in range(3):
        r_y(i).wait()
    q = jnp.zeros((NE, SEC), F32)
    for t in range(4):
        q = q + dot(rr[t], aos[t], 1, 0)
    q0[0] = q.astype(BF)
    for m in range(1, 8):
        q_zc(m).start()
    for i in range(3):
        rp(i).wait()
        back(i).wait()
    for t in range(4):
        more = dot(rrow, rpt[t], 0, 0)
        attn[:, t * SEC : (t + 1) * SEC] = (mr[t].astype(F32) + more).astype(BF)
    for m in range(1, 8):
        q_zc(m).wait()
    eight = [q0[m].astype(F32) for m in range(8)]
    while len(eight) > 1:
        eight = [eight[m] + eight[m + 1] for m in range(0, len(eight), 2)]
    q3[0] = eight[0].astype(BF)
    for i in range(3):
        q_x(i).start()
    for i in range(3):
        q_x(i).wait()
    qt[...] = four(q3)

    put(0, NA - 1).wait()
    put(1, NA + NC - 1).wait()
    put_tail().wait()
    h_core().wait()
    for i in range(2):
        for part in range(2):
            tok(part, i).wait_send()
            tok_f(part, i).wait_send()
    for i in range(3):
        sections(i).wait_send()
        g_z(i).wait_send()
        g_x(i).wait_send()
        h_x(i).wait_send()
        h_z(i).wait_send()
        s_x(i).wait_send()
    for part in range(2):
        for i in range(4):
            s_z(part, i).wait_send()
        for i in range(3):
            s_c(part, i).wait_send()

    @pl.loop(0, NA)
    def _(k):
        for i in range(4):
            a_z(k, i).wait_send()
        for i in range(3):
            a_c(k, i).wait_send()
            a_x(k, i).wait_send()
        for i in range(2):
            a_y(k, i).wait_send()
            a_f(k, i).wait_send()

    @pl.loop(0, NC)
    def _(j):
        for i in range(4):
            c_z(j, i).wait_send()
        for i in range(3):
            c_c(j, i).wait_send()

        @pl.when(j >= NC - 2)
        def _():
            for i in range(3):
                c_x(j, i).wait_send()


def local(
    out_grad, expert_ids, chosen_logits, router_weight, hidden_act, down_weight, attn_out, proj_weight
):
    vm = pl.BlockSpec(memory_space=pltpu.VMEM)
    hbm = pl.BlockSpec(memory_space=pl.ANY)
    sds = jax.ShapeDtypeStruct
    sem = pltpu.SemaphoreType.DMA
    v = pltpu.VMEM
    dg, total, _, _, attn, lg, qt = pl.pallas_call(
        kernel,
        out_shape=(
            sds((FF, D), BF), sds((SEC, D), BF), sds((NA, 16, 160, CH), BF),
            sds((NC, 4, 4, 160, CH), BF), sds((TOK, HID), BF), sds((4, TOK), F32),
            sds((NE, SEC), BF),
        ),
        in_specs=[hbm] * 8,
        out_specs=(hbm, hbm, hbm, hbm, vm, vm, vm),
        scratch_shapes=[
            v((D, TOK), BF), v((4, TOK), jnp.int32), v((4, TOK), F32), v((D, SEC), BF),
            v((NE, D), BF), v((2, 2, FF, TOK), BF), v((4, TOK, DP), BF),
            v((NA, 1024, CH), BF), v((NC, 4, 1024, CH), BF), v((4, 1024, 128), BF),
            v((4, 640, 1024), BF), v((NA, 4, 160, CH), BF), v((2, 4, 4, 160, CH), BF),
            v((4, 4, 160, 128), BF), v((4, 4, 160, 128), BF), v((2, 16, 160, CH), BF),
            v((FF, D), BF), v((16, 160, FF), BF), v((FF, ROWS), BF),
            v((ROWS, 128), F32), v((2, FF, CH), BF), v((FF, 64), BF),
            v((4, TOK, SEC), BF), v((SEC, SEC), BF), v((4, TOK, SEC), BF), v((4, TOK, SEC), BF),
            v((NE, SEC), BF), v((4, NE, SEC), BF), v((SEC, D), BF), v((256, D), BF),
            v((3, 64, D), BF), v((64, D), BF), v((3, 16, D), BF), v((64, D), BF),
            v((4, 4, 8, 128), F32), v((16, 8, 128), F32), v((4, 8, 128), F32),
            v((4, 4, 2, 8, 128), F32), v((4, NE, TOK), BF),
            v((8, NE, SEC), BF), v((4, NE, SEC), BF),
            sem((NA, 16)), sem((NA, 16)), sem((NC + 2, 16)), sem((NC + 2, 16)),
            sem((17,)), sem((17,)), sem((15,)), sem((15,)), sem((40,)), sem((40,)), sem((32,)),
        ],
        compiler_params=pltpu.CompilerParams(
            collective_id=0, has_side_effects=True, vmem_limit_bytes=62 * 2**20
        ),
        cost_estimate=pl.CostEstimate(
            flops=50 * 10**9, bytes_accessed=400 * 10**6, transcendentals=0
        ),
        name="layer_backward",
    )(
        out_grad.T, expert_ids.T, chosen_logits.T, attn_out, proj_weight.T, router_weight.T,
        jnp.transpose(hidden_act[0], (1, 2, 0)), down_weight[0],
    )
    more = dot(qt, router_weight, 0, 1)
    proj_grad = (total.astype(F32) + more).astype(BF)
    return attn, proj_grad, dg[None], lg.T


def solution(mesh):
    return jax.shard_map(
        local,
        mesh=mesh,
        in_specs=(
            P(("dp", "expert"), None),
            P(("dp", "expert"), None),
            P(("dp", "expert"), None),
            P(),
            P("expert", None, None, "dp"),
            P("expert", "dp", None),
            P(("dp", "expert"), None),
            P("dp", None),
        ),
        out_specs=(
            P(("dp", "expert"), None),
            P("dp", None),
            P("expert", "dp", None),
            P(("dp", "expert"), None),
        ),
        check_vma=False,
    )
```
